32 devices in a mesh: seq: 4 (over z), mp: 8 (over y, x, core).
Axes of the slice: x: 2, y: 2, z: 4, core: 2. Of those that a mesh axis runs over, the one named last changes fastest.
Arguments:
- tokens: bfloat16 [2, 4096, 1536], P(None, ('seq', 'mp')), may hold values from -6 to 6
- cotangent: bfloat16 [2, 4096, 1536], P(None, 'seq'), may hold values from -6 to 6
- w_x: bfloat16 [1536, 2048], P('seq', 'mp'), may hold values from -0.15625 to 0.15625
- w_y: bfloat16 [1536, 2048], P('seq', 'mp'), may hold values from -0.15625 to 0.15625
- w_out: bfloat16 [2048, 1536], P('mp', 'seq'), may hold values from -0.5 to 0.5
- w_gate: bfloat16 [1536, 4608], P('seq', 'mp'), may hold values from -0.15625 to 0.15625
- w_up: bfloat16 [1536, 4608], P('seq', 'mp'), may hold values from -0.15625 to 0.15625
- w_down: bfloat16 [4608, 1536], P('mp', 'seq'), may hold values from -0.1875 to 0.1875
- gate_a: bfloat16 [16, 128, 128], P('mp', 'seq'), may hold values from -0.5 to 0.5
- gate_i: bfloat16 [16, 128, 128], P('mp', 'seq'), may hold values from -0.5 to 0.5
- conv_w: bfloat16 [4, 2048], P(None, ('mp', 'seq')), may hold values from -2 to 2
- decay_param: bfloat16 [2048], P(('mp', 'seq'))
- bias_a: bfloat16 [2048], P(('mp', 'seq')), may hold values from -2 to 2
- bias_i: bfloat16 [2048], P(('mp', 'seq')), may hold values from -2 to 2
- gain_one: bfloat16 [1536], P('seq'), may hold values from 0.099609375 to 1.8984375
- gain_two: bfloat16 [1536], P('seq'), may hold values from 0.099609375 to 1.8984375
- doc_starts: int32 [2, 4], replicated, may hold values from 0 to 4095, as said below
Outputs:
- block_out: bfloat16 [2, 4096, 1536], P(None, ('seq', 'mp'))
- grad_tokens: bfloat16 [2, 4096, 1536], P(None, ('seq', 'mp'))
- grad_w_x: float32 [1536, 2048], P('seq', 'mp')
- grad_w_y: float32 [1536, 2048], P('seq', 'mp')
- grad_w_out: float32 [2048, 1536], P('mp', 'seq')
- grad_w_gate: float32 [1536, 4608], P('seq', 'mp')
- grad_w_up: float32 [1536, 4608], P('seq', 'mp')
- grad_w_down: float32 [4608, 1536], P('mp', 'seq')
- grad_gate_a: float32 [16, 128, 128], P('mp', 'seq')
- grad_gate_i: float32 [16, 128, 128], P('mp', 'seq')
- grad_conv_w: float32 [4, 2048], P(None, ('mp', 'seq'))
- grad_decay_param: float32 [2048], P(('mp', 'seq'))
- grad_bias_a: float32 [2048], P(('mp', 'seq'))
- grad_bias_i: float32 [2048], P(('mp', 'seq'))
- grad_gain_one: float32 [1536], P('seq')
- grad_gain_two: float32 [1536], P('seq')
The draws below stay inside these ranges and needn't reach their ends.
Inputs may be any that keep to these rules, and one draw needn't show every extreme that they name: `doc_starts`: an entry is a stream position at which a document starts; an entry 0 marks nothing and entries may repeat. In one micro-batch, drawn from the seed, every entry is 0.
All inputs are finite; a program needn't handle non-finite values.
Results may differ from the reference program's by a relative error of at most 0.025.
Values may be sent and summed in bfloat16 or wider, within the bound.
No kernel may reach another device: no remote copies, remote signals or barrier semaphores. Data moves between devices by JAX's collectives and lax.ppermute only.
A program may use at most 128 MiB of HBM per device.

```python
import math
import jax
import jax.numpy as jnp
from jax import lax

D = 1536
LRU = 2048
BLOCKS = 16
FF = 4608
CONV = 4
MB = 2
STARTS = 4
TOKENS = 4096
BW = 128


def draw_decay_param(key, part):
    picker = jax.random.uniform(jax.random.fold_in(key, 11), (LRU,), jnp.float32)
    level = jax.random.uniform(jax.random.fold_in(key, 12), (LRU,), jnp.float32)
    slow_low = math.log(0.05 / TOKENS)
    slow_high = math.log(0.5 / TOKENS)
    fast_low = math.log(1.0 / TOKENS)
    fast_high = math.log(0.02)
    share = 0.5
    slow_rate = jnp.exp(slow_low + level * (slow_high - slow_low))
    fast_rate = jnp.exp(fast_low + level * (fast_high - fast_low))
    rates = jnp.where(picker < share, slow_rate, fast_rate)
    return jnp.log(jnp.expm1(rates)).astype(jnp.bfloat16)


def draw_doc_starts(key, part):
    long_one = jax.random.randint(jax.random.fold_in(key, 21), (), 0, MB)
    spots = jax.random.randint(jax.random.fold_in(key, 22), (MB, STARTS), 1, TOKENS)
    row_ids = jnp.arange(MB, dtype=jnp.int32)[:, None]
    col_ids = jnp.arange(STARTS, dtype=jnp.int32)[None, :]
    edge_row = (long_one + 1) % MB
    spots = jnp.where((row_ids == edge_row) & (col_ids == 0), TOKENS - 1, spots)
    return jnp.where(row_ids == long_one, 0, spots).astype(jnp.int32)


def shard_levels(stream_key, dims, split, least, top_value):
    factor_of = 1.0
    for dim, parts in split:
        steps = jax.random.uniform(jax.random.fold_in(jax.random.fold_in(stream_key, 6), dim), (parts,), jnp.float32, least / len(split), top_value / len(split))
        factor_of = factor_of * jnp.repeat(jnp.exp(steps), dims[dim] // parts).reshape((-1,) + (1,) * (len(dims) - 1 - dim))
    return factor_of


def scatter_about(stream_key, dims, spread, bound, cuts=(), kind=jnp.bfloat16):
    values = spread * jax.random.normal(stream_key, dims, jnp.float32)
    if cuts:
        values = values * shard_levels(stream_key, dims, cuts, -0.22, 0.18)
    return jnp.clip(values, -bound, bound).astype(kind)


def setup_inputs(seed: int = 0) -> dict:
    arg_keys = jax.random.split(jax.random.key(seed), 18)
    return {
        "tokens": scatter_about(arg_keys[0], (MB, TOKENS, D), 1.0, 6.0, ((1, 32),)),
        "cotangent": scatter_about(arg_keys[1], (MB, TOKENS, D), 1.0, 6.0, ((1, 4),)),
        "w_x": scatter_about(arg_keys[2], (D, LRU), D ** -0.5, 0.15625, ((0, 4), (1, 8))),
        "w_y": scatter_about(arg_keys[3], (D, LRU), D ** -0.5, 0.15625, ((0, 4), (1, 8))),
        "w_out": scatter_about(arg_keys[4], (LRU, D), (LRU // 16) ** -0.5, 0.5, ((0, 8), (1, 4))),
        "w_gate": scatter_about(arg_keys[5], (D, FF), D ** -0.5, 0.15625, ((0, 4), (1, 8))),
        "w_up": scatter_about(arg_keys[6], (D, FF), D ** -0.5, 0.15625, ((0, 4), (1, 8))),
        "w_down": scatter_about(arg_keys[7], (FF, D), (FF // 4) ** -0.5, 0.1875, ((0, 8), (1, 4))),
        "gate_a": scatter_about(arg_keys[8], (BLOCKS, BW, BW), BW ** -0.5, 0.5, ((0, 8), (1, 4))),
        "gate_i": scatter_about(arg_keys[9], (BLOCKS, BW, BW), BW ** -0.5, 0.5, ((0, 8), (1, 4))),
        "conv_w": scatter_about(arg_keys[10], (CONV, LRU), 0.5, 2.0, ((1, 32),)),
        "decay_param": draw_decay_param(jax.random.fold_in(arg_keys[17], 71), 0),
        "bias_a": scatter_about(arg_keys[12], (LRU,), 0.5, 2.0, ((0, 32),)),
        "bias_i": scatter_about(arg_keys[13], (LRU,), 0.5, 2.0, ((0, 32),)),
        "gain_one": jnp.clip(1.0 + 0.18 * jax.random.normal(arg_keys[14], (D,), jnp.float32), 0.099609375, 1.8984375).astype(jnp.bfloat16),
        "gain_two": jnp.clip(1.0 + 0.18 * jax.random.normal(arg_keys[15], (D,), jnp.float32), 0.099609375, 1.8984375).astype(jnp.bfloat16),
        "doc_starts": draw_doc_starts(jax.random.fold_in(arg_keys[17], 71), 0),
    }


epsilon = 1e-06

@jax.custom_vjp
def low(v):
    return lax.optimization_barrier(v.astype(jnp.bfloat16)).astype(jnp.float32)

@jax.custom_vjp
def low_back(v):
    return v

def low_keep(v):
    return (low(v), None)

def low_pass(kept, grad):
    return (grad,)

def back_keep(v):
    return (v, None)

def back_low(kept, grad):
    return (low(grad),)
low.defvjp(low_keep, low_pass)
low_back.defvjp(back_keep, back_low)

def matmul(left_mat, right_mat):
    return jnp.dot(left_mat, right_mat, precision=lax.Precision.HIGHEST)

def gelu_tanh(values):
    return jax.nn.gelu(values, approximate=True)

def rms_scale(values, gain_vec):
    return values * lax.rsqrt(lax.optimization_barrier(jnp.mean(values * values, axis=-1, keepdims=True)) + epsilon) * gain_vec

def combine_pairs(former, latter):
    return (former[0] * latter[0], latter[0] * former[1] + latter[1])

def conv_mix(padded, conv_taps, tap_masks):
    length = tap_masks.shape[1]
    tap_count = conv_taps.shape[0]
    running = jnp.zeros((length, padded.shape[1]), jnp.float32)
    for offset in range(tap_count):
        window = lax.slice_in_dim(padded, tap_count - 1 - offset, tap_count - 1 - offset + length, axis=0)
        running = running + conv_taps[offset] * window * tap_masks[offset]
    return running

def gate_terms(conv_out, rate_mat, rate_shift, input_mat, input_shift, decay_in, resets):
    length = conv_out.shape[0]
    groups = rate_mat.shape[0]
    group_width = rate_mat.shape[2]
    blocks = conv_out.reshape(length, groups, group_width)
    rate_pre = jnp.einsum('tnc,ncd->tnd', blocks, rate_mat, precision=lax.Precision.HIGHEST).reshape(length, groups * group_width) + rate_shift
    input_pre = jnp.einsum('tnc,ncd->tnd', blocks, input_mat, precision=lax.Precision.HIGHEST).reshape(length, groups * group_width) + input_shift
    rate_gate = jax.nn.sigmoid(rate_pre)
    input_gate = jax.nn.sigmoid(input_pre)
    log_decay = -8.0 * jax.nn.softplus(decay_in) * rate_gate
    keeps = jnp.exp(log_decay) * (1.0 - resets)
    inflow = jnp.sqrt(-jnp.expm1(2.0 * log_decay)) * input_gate * conv_out
    return (keeps, inflow)

def doc_masks(starts_row, first_pos, length, tap_count):
    active = starts_row > 0
    positions = first_pos + jnp.arange(length, dtype=jnp.int32)

    def counted(places):
        return lax.optimization_barrier(jnp.sum((active[None, :] & (starts_row[None, :] <= places[:, None])).astype(jnp.int32), axis=1))
    current = counted(positions)
    tap_masks = jnp.stack([(counted(positions - offset) == current).astype(jnp.float32)[:, None] for offset in range(tap_count)])
    resets = jnp.any(starts_row[None, :] == positions[:, None], axis=1).astype(jnp.float32)[:, None]
    return (tap_masks, resets)

def block(params, stream, tap_masks, resets):
    w_x, w_y, w_out, w_gate, w_up, w_down, gate_a, gate_i, conv_w, decay_param, bias_a, bias_i, gain_one, gain_two = params
    normed = low(rms_scale(stream, gain_one))
    lru_in = low_back(matmul(normed, w_x))
    branch_pre = low_back(matmul(normed, w_y))
    tap_count = conv_w.shape[0]
    padded = jnp.concatenate([jnp.zeros((tap_count - 1, lru_in.shape[1]), jnp.float32), lru_in], axis=0)
    conv_out = conv_mix(padded, conv_w, tap_masks)
    keeps, inflow = gate_terms(conv_out, gate_a, bias_a, gate_i, bias_i, decay_param, resets)
    states = lax.associative_scan(combine_pairs, (keeps, inflow))[1]
    mixed_out = low(states * gelu_tanh(branch_pre))
    middle = stream + low_back(matmul(mixed_out, w_out))
    normed_two = low(rms_scale(middle, gain_two))
    gate_pre = low_back(matmul(normed_two, w_gate))
    up_pre = low_back(matmul(normed_two, w_up))
    hidden = low(gelu_tanh(gate_pre) * up_pre)
    return middle + low_back(matmul(hidden, w_down))

def reference(tokens, cotangent, w_x, w_y, w_out, w_gate, w_up, w_down, gate_a, gate_i, conv_w, decay_param, bias_a, bias_i, gain_one, gain_two, doc_starts):
    params = tuple((weight.astype(jnp.float32) for weight in (w_x, w_y, w_out, w_gate, w_up, w_down, gate_a, gate_i, conv_w, decay_param, bias_a, bias_i, gain_one, gain_two)))

    def micro_step(running, inputs_now):
        stream, cot_rows, starts_row = inputs_now
        tap_masks, resets = doc_masks(starts_row, 0, TOKENS, CONV)

        def forward(weights, inputs):
            return block(weights, inputs, tap_masks, resets)
        output, pullback = jax.vjp(forward, params, stream.astype(jnp.float32))
        grad_params, grad_stream = pullback(cot_rows.astype(jnp.float32))
        running = tuple((earlier_sum + gradient for earlier_sum, gradient in zip(running, grad_params)))
        return (running, (output.astype(jnp.bfloat16), grad_stream.astype(jnp.bfloat16)))
    initial = tuple((jnp.zeros_like(weight) for weight in params))
    sums, outputs = lax.scan(micro_step, initial, (tokens, cotangent, doc_starts))
    return (outputs[0], outputs[1], sums[0], sums[1], sums[2], sums[3], sums[4], sums[5], sums[6], sums[7], sums[8], sums[9], sums[10], sums[11], sums[12], sums[13])
```

```python
import functools

import jax
import jax.numpy as jnp
from jax import lax
from jax.experimental import pallas as pl
from jax.experimental.pallas import tpu as pltpu
from jax.sharding import PartitionSpec as P

epsilon = 1e-06
SEGS = 8
WIDE = 128
TILE = 128
ROOT = 0.7978845608028654
CUBE = 0.044715


def gelu_pair(v):
    inner = ROOT * v * (1.0 + CUBE * v * v)
    t = jnp.tanh(inner)
    half = 0.5 * (1.0 + t)
    slope = half + 0.5 * v * (1.0 - t * t) * (ROOT * (1.0 + (3.0 * CUBE) * v * v))
    return v * half, slope


def gelu_only(v):
    return v * (0.5 + 0.5 * jnp.tanh(ROOT * v * (1.0 + CUBE * v * v)))


def swapped(x, flips):
    rows = lax.broadcasted_iota(jnp.int32, x.shape, 0)
    for bit in (1, 2, 4):
        down, up = pltpu.roll(x, SEGS - bit, 0), pltpu.roll(x, bit, 0)
        turned = jnp.where((rows & bit) == 0, down, up)
        x = jnp.where((flips & bit) != 0, turned, x)
    return x


def exclusive(prod, last, flips, backward):
    prod, last = swapped(prod, flips), swapped(last, flips)
    one = jnp.ones((1, WIDE), jnp.float32)
    zero = jnp.zeros((1, WIDE), jnp.float32)
    coef, base = [one], [zero]
    order = range(SEGS - 1, -1, -1) if backward else range(SEGS)
    for s in order:
        coef.append(prod[s : s + 1] * coef[-1])
        base.append(prod[s : s + 1] * base[-1] + last[s : s + 1])
    total = jnp.concatenate([coef[-1], base[-1]] + [zero] * (SEGS - 2), axis=0)
    coef, base = coef[:-1], base[:-1]
    if backward:
        coef, base = coef[::-1], base[::-1]
    return (
        swapped(jnp.concatenate(coef, axis=0), flips),
        swapped(jnp.concatenate(base, axis=0), flips),
        total,
    )


def enter_kernel(
    where, u, edge, code, small, gates, inter, v_out, rg_out, ig_out, e_out, sq_out, maps, total
):
    rows = u.shape[0]
    steps = rows // SEGS
    flips = where[0]

    def lay(s, carry):
        inter[pl.ds(pl.multiple_of(24 + 8 * s, 8), 8), :] = u[pl.ds(s, 8, stride=steps), :]
        return carry

    lax.fori_loop(0, steps, lay, 0, unroll=8)
    first = lax.broadcasted_iota(jnp.int32, (SEGS, WIDE), 0) == 0
    for j in range(3):
        nat = pltpu.roll(swapped(inter[pl.ds(8 * (steps + j), 8), :], flips), 1, 0)
        nat = jnp.where(first, edge[5 + j : 6 + j, :], nat)
        inter[8 * j : 8 * j + 8, :] = swapped(nat, flips)

    def tile(i, carry):
        prod, state = carry
        base = pl.multiple_of(i * TILE, TILE)
        c = code[pl.ds(base, TILE), :]
        v = small[0:1, :] * inter[pl.ds(base + 24, TILE), :]
        for k in (1, 2, 3):
            v = v + jnp.where(
                c >= k, small[k : k + 1, :] * inter[pl.ds(base + 24 - 8 * k, TILE), :], 0.0
            )
        high = v.astype(jnp.bfloat16)
        low = (v - high.astype(jnp.float32)).astype(jnp.bfloat16)
        mat = gates[0]
        pre = jnp.dot(
            jnp.concatenate([high, low], axis=1),
            jnp.concatenate([mat, mat], axis=0),
            preferred_element_type=jnp.float32,
        )
        rg = 1.0 / (1.0 + jnp.exp(-(pre[:, :WIDE] + small[5:6, :])))
        ig = jax.nn.sigmoid(pre[:, WIDE:] + small[6:7, :])
        la = small[4:5, :] * rg
        e = jnp.exp(la)
        sq = jnp.sqrt(jnp.tanh(-la) * (1.0 + e * e))
        here = pl.ds(base, TILE)
        v_out[here, :] = v
        rg_out[here, :] = rg
        ig_out[here, :] = ig
        e_out[here, :] = e
        sq_out[here, :] = sq
        keep = jnp.where(c > 0, e, 0.0)
        inflow = sq * ig * v
        for s in range(TILE // SEGS):
            k = keep[8 * s : 8 * s + 8]
            prod = prod * k
            state = k * state + inflow[8 * s : 8 * s + 8]
        return prod, state

    prod, state = lax.fori_loop(
        0,
        rows // TILE,
        tile,
        (jnp.ones((SEGS, WIDE), jnp.float32), jnp.zeros((SEGS, WIDE), jnp.float32)),
    )
    coef, base, whole = exclusive(prod, state, flips, False)
    maps[0:8, :] = prod
    maps[8:16, :] = coef
    maps[16:24, :] = base
    total[...] = whole


def state_kernel(count, where, v, ig, e, sq, code, p, maps, *rest):
    others, (hs, out, wide) = rest[: count - 1], rest[count - 1 :]
    rows = v.shape[0]
    steps = rows // SEGS
    mine = where[1]
    entry = jnp.zeros((1, WIDE), jnp.float32)
    for d in range(count - 1, 0, -1):
        piece = others[d - 1]
        entry = jnp.where(mine >= d, piece[0:1, :] * entry + piece[1:2, :], entry)
    state = maps[8:16, :] * entry + maps[16:24, :]
    hs[0:8, :] = state

    def tile(i, state):
        base = pl.multiple_of(i * TILE, TILE)
        here = pl.ds(base, TILE)
        keep = jnp.where(code[here, :] > 0, e[here, :], 0.0)
        inflow = sq[here, :] * ig[here, :] * v[here, :]
        for s in range(TILE // SEGS):
            state = keep[8 * s : 8 * s + 8] * state + inflow[8 * s : 8 * s + 8]
            hs[pl.ds(base + 8 * s + 8, 8), :] = state
            there = pl.ds(i * (TILE // SEGS) + s, 8, stride=steps)
            wide[there, :] = state * gelu_only(p[there, :])
        return state

    lax.fori_loop(0, rows // TILE, tile, state)
    out[...] = wide[...].astype(jnp.bfloat16)


def adjoint_kernel(where, do, p, hs, e, code, maps, dhs, dp, back, total, wide):
    rows = do.shape[0]
    steps = rows // SEGS
    flips = where[0]

    def tile(i, grad):
        i = rows // TILE - 1 - i
        base = pl.multiple_of(i * TILE, TILE)
        keep = jnp.where(code[pl.ds(base, TILE), :] > 0, e[pl.ds(base, TILE), :], 0.0)
        for s in range(TILE // SEGS - 1, -1, -1):
            there = pl.ds(i * (TILE // SEGS) + s, 8, stride=steps)
            d = do[there, :]
            act, slope = gelu_pair(p[there, :])
            wide[there, :] = d * hs[pl.ds(base + 8 * s + 8, 8), :] * slope
            dh = d * act
            dhs[pl.ds(base + 8 * s, 8), :] = dh
            grad = keep[8 * s : 8 * s + 8] * (dh + grad)
        return grad

    grad = lax.fori_loop(0, rows // TILE, tile, jnp.zeros((SEGS, WIDE), jnp.float32))
    dp[...] = wide[...].astype(jnp.bfloat16)
    coef, base, whole = exclusive(maps[0:8, :], grad, flips, True)
    back[0:8, :] = coef
    back[8:16, :] = base
    total[...] = whole


def leave_kernel(count, where, dhs, inter, v, rg, ig, e, sq, hs, code, small, gates_t, back, *rest):
    products, grads = rest[: count - 1], rest[count - 1 : 2 * count - 2]
    du, grad_gates, sums, edge, dv_all, wide = rest[2 * count - 2 :]
    rows = dhs.shape[0]
    steps = rows // SEGS
    flips, mine = where[0], where[1]
    entry = jnp.zeros((1, WIDE), jnp.float32)
    for j in range(count - 1, 0, -1):
        d = count - j
        entry = jnp.where(
            mine + j < count, products[d - 1][0:1, :] * entry + grads[d - 1][1:2, :], entry
        )
    grad = back[0:8, :] * entry + back[8:16, :]
    grad_gates[...] = jnp.zeros_like(grad_gates)

    def fold(x):
        parts = [x[8 * s : 8 * s + 8] for s in range(TILE // SEGS)]
        while len(parts) > 1:
            parts = [a + b for a, b in zip(parts[::2], parts[1::2])]
        return parts[0]

    def tile(i, carry):
        grad, taps, decay, shift_a, shift_i = carry
        i = rows // TILE - 1 - i
        base = pl.multiple_of(i * TILE, TILE)
        here = pl.ds(base, TILE)
        c = code[here, :]
        e_now, sq_now, rg_now, ig_now, v_now = e[here, :], sq[here, :], rg[here, :], ig[here, :], v[here, :]
        keep = jnp.where(c > 0, e_now, 0.0)
        d_now = dhs[here, :]
        pieces = [None] * (TILE // SEGS)
        for s in range(TILE // SEGS - 1, -1, -1):
            a = d_now[8 * s : 8 * s + 8] + grad
            pieces[s] = a
            grad = keep[8 * s : 8 * s + 8] * a
        a = jnp.concatenate(pieces, axis=0)
        q = ig_now * v_now
        dla = a * (keep * hs[here, :] - q * (e_now * e_now) / jnp.maximum(sq_now, 1e-25))
        rate = rg_now * dla
        decay = decay + fold(rate)
        dra = small[4:5, :] * rate * (1.0 - rg_now)
        asq = a * sq_now
        dia = asq * q * (1.0 - ig_now)
        shift_a = shift_a + fold(dra)
        shift_i = shift_i + fold(dia)
        both = jnp.concatenate([dra.astype(jnp.bfloat16), dia.astype(jnp.bfloat16)], axis=1)
        dv = asq * ig_now + jnp.dot(both, gates_t[0], preferred_element_type=jnp.float32)
        grad_gates[0] += lax.dot_general(
            v_now.astype(jnp.bfloat16),
            both,
            (((0,), (0,)), ((), ())),
            preferred_element_type=jnp.float32,
        )
        dv_all[here, :] = dv
        new_taps = [taps[0] + fold(dv * inter[pl.ds(base + 24, TILE), :])]
        for k in (1, 2, 3):
            new_taps.append(
                taps[k]
                + fold(jnp.where(c >= k, dv * inter[pl.ds(base + 24 - 8 * k, TILE), :], 0.0))
            )
        return grad, tuple(new_taps), decay, shift_a, shift_i

    zero = jnp.zeros((SEGS, WIDE), jnp.float32)
    _, taps, decay, shift_a, shift_i = lax.fori_loop(
        0, rows // TILE, tile, (grad, (zero,) * 4, zero, zero, zero)
    )
    totals = [jnp.sum(x, axis=0, keepdims=True) for x in (*taps, decay, shift_a, shift_i)]
    sums[...] = jnp.concatenate(totals + [jnp.zeros((1, WIDE), jnp.float32)], axis=0)
    last = lax.broadcasted_iota(jnp.int32, (SEGS, WIDE), 0) == SEGS - 1
    edges = []
    for j in range(3):
        nat = swapped(dv_all[8 * j : 8 * j + 8, :], flips)
        edges.append(nat[0:1])
        nat = jnp.where(last, 0.0, pltpu.roll(nat, SEGS - 1, 0))
        dv_all[pl.ds(rows + 8 * j, 8), :] = swapped(nat, flips)
    edge[...] = jnp.concatenate(edges + [jnp.zeros((SEGS - 3, WIDE), jnp.float32)], axis=0)

    def mix(i, carry):
        base = pl.multiple_of(i * TILE, TILE)
        total = small[0:1, :] * dv_all[pl.ds(base, TILE), :]
        for k in (1, 2, 3):
            there = pl.ds(base + 8 * k, TILE)
            total = total + jnp.where(
                code[there, :] >= k, small[k : k + 1, :] * dv_all[there, :], 0.0
            )
        for s in range(TILE // SEGS):
            wide[pl.ds(i * (TILE // SEGS) + s, 8, stride=steps), :] = total[8 * s : 8 * s + 8]
        return carry

    lax.fori_loop(0, rows // TILE, mix, 0)
    du[...] = wide[...].astype(jnp.bfloat16)


def lanes(rows, offset=0):
    return pl.BlockSpec((rows, WIDE), lambda n: (0, n + offset))


def per_block(shape):
    return pl.BlockSpec((1,) + shape, lambda n: (n, 0, 0))


def scalars():
    return pl.BlockSpec(memory_space=pltpu.SMEM)


def shared(shape):
    return pl.BlockSpec(shape, lambda n: (0,) * len(shape))


def launch(kernel, groups, in_specs, outs, scratch, args, ops, name):
    moved = sum(a.size * a.dtype.itemsize for a in args) + sum(
        functools.reduce(lambda x, y: x * y, s, 1) * jnp.dtype(t).itemsize for s, t, _ in outs
    )
    return pl.pallas_call(
        kernel,
        grid=(groups,),
        in_specs=in_specs,
        out_specs=[spec for _, _, spec in outs],
        out_shape=[jax.ShapeDtypeStruct(shape, dtype) for shape, dtype, _ in outs],
        scratch_shapes=scratch,
        compiler_params=pltpu.CompilerParams(vmem_limit_bytes=40 * 2**20),
        cost_estimate=pl.CostEstimate(flops=ops, bytes_accessed=moved, transcendentals=ops // 20),
        name=name,
    )(*args)


def enter(where, both, edge, code, small, gates):
    rows, channels = both.shape[0], both.shape[1] // 2
    groups = channels // WIDE
    f32 = jnp.float32
    full = ((rows, channels), f32, lanes(rows))
    return launch(
        enter_kernel,
        groups,
        [scalars(), lanes(rows), lanes(8), shared(code.shape), lanes(8), per_block((WIDE, 2 * WIDE))],
        [
            ((rows + 24, channels), f32, lanes(rows + 24)),
            full,
            full,
            full,
            full,
            full,
            ((24, channels), f32, lanes(24)),
            ((8, channels), f32, lanes(8)),
        ],
        [],
        (where, both, edge, code, small, gates),
        rows * channels * 600,
        "enter",
    )


def states_of(where, v, ig, e, sq, code, both, maps, others):
    rows, channels = v.shape
    groups = channels // WIDE
    f32 = jnp.float32
    return launch(
        functools.partial(state_kernel, len(others) + 1),
        groups,
        [scalars()]
        + [lanes(rows)] * 4
        + [shared(code.shape), lanes(rows, groups), lanes(24)]
        + [lanes(8)] * len(others),
        [
            ((rows + 8, channels), f32, lanes(rows + 8)),
            ((rows, channels), jnp.bfloat16, lanes(rows)),
        ],
        [pltpu.VMEM((rows, WIDE), f32)],
        (where, v, ig, e, sq, code, both, maps, *others),
        rows * channels * 60,
        "states",
    )


def adjoints(where, do, both, hs, e, code, maps):
    rows, channels = do.shape
    groups = channels // WIDE
    f32 = jnp.float32
    return launch(
        adjoint_kernel,
        groups,
        [
            scalars(),
            lanes(rows),
            lanes(rows, groups),
            lanes(rows + 8),
            lanes(rows),
            shared(code.shape),
            lanes(24),
        ],
        [
            ((rows, channels), f32, lanes(rows)),
            ((rows, channels), jnp.bfloat16, lanes(rows)),
            ((16, channels), f32, lanes(16)),
            ((8, channels), f32, lanes(8)),
        ],
        [pltpu.VMEM((rows, WIDE), f32)],
        (where, do, both, hs, e, code, maps),
        rows * channels * 80,
        "adjoint",
    )


def leave(where, dhs, kept, hs, code, small, gates_t, back, products, grads):
    inter, v, rg, ig, e, sq = kept
    rows, channels = dhs.shape
    groups = channels // WIDE
    f32 = jnp.float32
    count = len(products) + 1
    return launch(
        functools.partial(leave_kernel, count),
        groups,
        [scalars(), lanes(rows), lanes(rows + 24)]
        + [lanes(rows)] * 5
        + [
            lanes(rows + 8),
            shared(code.shape),
            lanes(8),
            per_block((2 * WIDE, WIDE)),
            lanes(16),
        ]
        + [lanes(8)] * (2 * count - 2),
        [
            ((rows, channels), jnp.bfloat16, lanes(rows)),
            ((groups, WIDE, 2 * WIDE), f32, per_block((WIDE, 2 * WIDE))),
            ((8, channels), f32, lanes(8)),
            ((8, channels), f32, lanes(8)),
        ],
        [pltpu.VMEM((rows + 24, WIDE), f32), pltpu.VMEM((rows, WIDE), f32)],
        (where, dhs, inter, v, rg, ig, e, sq, hs, code, small, gates_t, back, *products, *grads),
        rows * channels * 900,
        "leave",
    )


def dense(left_mat, right_mat):
    return jnp.dot(left_mat, right_mat, preferred_element_type=jnp.float32)


def dense_nt(left_mat, right_mat):
    return lax.dot_general(
        left_mat, right_mat, (((1,), (1,)), ((), ())), preferred_element_type=jnp.float32
    )


def dense_tn(left_mat, right_mat):
    return lax.dot_general(
        left_mat, right_mat, (((0,), (0,)), ((), ())), preferred_element_type=jnp.float32
    )


def low(x):
    return x.astype(jnp.bfloat16)


def turned(x, axis, distance):
    count = lax.axis_size(axis)
    return lax.ppermute(x, axis, [(i, (i + distance) % count) for i in range(count)])


def around(x, axis):
    return [turned(x, axis, d) for d in range(1, lax.axis_size(axis))]


def flip(x, bits):
    count = lax.axis_size("mp")
    return lax.ppermute(x, "mp", [(i, i ^ bits) for i in range(count)])


class Paired:
    halves = 2

    def spread(self, rows):
        return jnp.concatenate([rows] + [flip(rows, bits) for bits in (2, 4, 6)], axis=0)

    def collect(self, count, part):
        size = count // 4
        blocks = [slice(size * b, size * (b + 1)) for b in range(4)]
        far = [flip(low(part(blocks[b])), 2 * b) for b in (3, 1, 2)]
        total = part(blocks[0])
        for piece in far:
            total = total + piece.astype(jnp.float32)
        return total

    def both(self, x, axis):
        return jnp.concatenate([x, flip(x, 1)], axis=axis)

    def own_sum(self, x, axis):
        size = x.shape[axis] // 2
        mine = lax.slice_in_dim(x, 0, size, axis=axis)
        other = low(lax.slice_in_dim(x, size, 2 * size, axis=axis))
        return mine + flip(other, 1).astype(jnp.float32)


class Plain:
    halves = 1

    def spread(self, rows):
        return lax.all_gather(rows, "mp", axis=0, tiled=True)

    def collect(self, count, part):
        return lax.psum_scatter(
            low(part(slice(0, count))), "mp", scatter_dimension=0, tiled=True
        ).astype(jnp.float32)

    def both(self, x, axis):
        return x

    def own_sum(self, x, axis):
        return x


def mask_code(starts_row, first_pos, flips, steps):
    segs = lax.broadcasted_iota(jnp.int32, (steps + 3, SEGS), 1)
    step = lax.broadcasted_iota(jnp.int32, (steps + 3, SEGS), 0)
    places = first_pos + (segs ^ flips) * steps + step
    code = jnp.full(places.shape, 4, jnp.int32)
    for e in range(starts_row.shape[0]):
        start = starts_row[e]
        code = jnp.where(
            (start > 0) & (places >= start), jnp.minimum(code, places - start), code
        )
    code = code.astype(jnp.float32).reshape(-1, 1)
    return jnp.broadcast_to(code, (code.shape[0], WIDE))


def normed(rows):
    scale = lax.rsqrt(jnp.mean(rows * rows, axis=-1, keepdims=True) + epsilon)
    return rows * scale, scale


def norm_back(grad_norm, norm, scale):
    return scale * (grad_norm - norm * jnp.mean(grad_norm * norm, axis=-1, keepdims=True))


def micro(plan, where, flips, stream, cot, cot_rows, starts_row, weights):
    wx, wy, wo, wg, wu, wd, gates, taps, decay, shift_a, shift_i, gain_one, gain_two = weights
    count = cot.shape[0]
    steps = count // SEGS
    seq_rank = lax.axis_index("seq")
    channels = wo.shape[0]
    hidden = wd.shape[0]
    code = mask_code(starts_row, seq_rank * count, flips, steps)
    rate = -8.0 * jax.nn.softplus(decay)
    small = jnp.concatenate(
        [taps, rate[None], shift_a[None], shift_i[None], jnp.zeros((1, channels), jnp.float32)],
        axis=0,
    )
    gates_t = jnp.concatenate(
        [gates[:, :, :WIDE].transpose(0, 2, 1), gates[:, :, WIDE:].transpose(0, 2, 1)], axis=1
    )

    n1, s1 = normed(stream)
    h1 = plan.spread(low(n1 * gain_one))
    last = lax.dynamic_slice_in_dim(h1, ((SEGS - 1) ^ flips) * steps + steps - 8, 8, 0)
    before = turned(last, "seq", 1)
    edge = jnp.where(seq_rank > 0, dense_nt(before, wx), 0.0)
    up_both = dense_nt(h1, jnp.concatenate([wx, wy], axis=0))
    *kept, maps, total = enter(where, up_both, edge, code, small, gates)
    inter, v, rg, ig, e, sq = kept
    fore = around(total, "seq")
    hs, mixed = states_of(where, v, ig, e, sq, code, up_both, maps, fore)

    middle = stream + plan.collect(count, lambda rows: dense(mixed[rows], wo))
    n2, s2 = normed(middle)
    h2 = plan.spread(low(n2 * gain_two))
    gate_pre = dense_nt(h2, wg)
    up_pre = dense_nt(h2, wu)
    act, slope = gelu_pair(gate_pre)
    mid = low(act * up_pre)
    grad_mid = dense_nt(cot, wd)
    low_gate = low(grad_mid * up_pre * slope)
    low_up = low(grad_mid * act)

    back_two = plan.collect(
        count, lambda rows: dense(low_gate[rows], wg) + dense(low_up[rows], wu)
    )
    block_rows = low(middle + plan.collect(count, lambda rows: dense(mid[rows], wd)))
    grad_wd = dense_tn(mid, cot)
    grad_wg = dense_tn(low_gate, h2)
    grad_wu = dense_tn(low_up, h2)
    grad_middle = cot_rows + norm_back(back_two * gain_two, n2, s2)
    mid_rows = plan.spread(low(grad_middle))
    do = dense_nt(mid_rows, wo)
    grad_wo = dense_tn(mixed, mid_rows)
    dhs, dp, back, total = adjoints(where, do, up_both, hs, e, code, maps)
    aft = around(total, "seq")
    du, grad_gates, sums, edge = leave(
        where, dhs, kept, hs, code, small, gates_t, back, fore, aft
    )
    nxt = jnp.where(
        seq_rank < lax.axis_size("seq") - 1, turned(edge, "seq", -1), 0.0
    )
    own = ((SEGS - 1) ^ flips) * steps
    after = seq_rank * count + count
    far = jnp.full((3,), 4, jnp.int32)
    for i in range(starts_row.shape[0]):
        places = after + jnp.arange(3, dtype=jnp.int32)
        start = starts_row[i]
        far = jnp.where((start > 0) & (places >= start), jnp.minimum(far, places - start), far)
    extra = []
    for j in range(3):
        row = jnp.zeros((channels,), jnp.float32)
        for k in range(3 - j, 4):
            row = row + jnp.where(far[j + k - 3] >= k, taps[k] * nxt[j + k - 3], 0.0)
        extra.append(row)
    extra = jnp.concatenate([jnp.zeros((5, channels), jnp.float32), jnp.stack(extra)], axis=0)
    at = own + steps - 8
    patch = low(lax.dynamic_slice_in_dim(du, at, 8, 0).astype(jnp.float32) + extra)
    du = lax.dynamic_update_slice_in_dim(du, patch, at, 0)
    back_one = plan.collect(count, lambda rows: dense(du[rows], wx) + dense(dp[rows], wy))
    grad_wx = dense_tn(du, h1)
    grad_wy = dense_tn(dp, h1)
    grad_rows = low(grad_middle + norm_back(back_one * gain_one, n1, s1))
    grad_one = (
        jnp.sum(grad_wx * wx.astype(jnp.float32) + grad_wy * wy.astype(jnp.float32), axis=0)
        / gain_one
    )
    grad_two = (
        jnp.sum(grad_wg * wg.astype(jnp.float32) + grad_wu * wu.astype(jnp.float32), axis=0)
        / gain_two
    )
    large = (grad_wx, grad_wy, grad_wo, grad_wg, grad_wu, grad_wd)
    decay_sum = -8.0 * jax.nn.sigmoid(decay) * sums[4]
    lines = jnp.concatenate([sums[:4], decay_sum[None], sums[5:7]], axis=0)
    return block_rows, grad_rows, large, (grad_gates, lines, jnp.stack([grad_one, grad_two]))


def on_device(
    tokens,
    cotangent,
    w_x,
    w_y,
    w_out,
    w_gate,
    w_up,
    w_down,
    gate_a,
    gate_i,
    conv_w,
    decay_param,
    bias_a,
    bias_i,
    gain_one,
    gain_two,
    doc_starts,
):
    micros, own_rows, _ = tokens.shape
    span = cotangent.shape[1]
    count = lax.axis_size("seq")
    seq_rank = lax.axis_index("seq")
    mp_rank = lax.axis_index("mp")
    paired = micros == 2 and lax.axis_size("mp") == SEGS and span == SEGS * own_rows
    plan = Paired() if paired else Plain()
    channels, hidden = w_x.shape[1], w_gate.shape[1]
    blocks, depth, _ = gate_a.shape
    part = w_x.shape[0]
    thin = conv_w.shape[1]

    flat = jnp.concatenate(
        [a.reshape(-1) for a in (gate_a, gate_i, conv_w, decay_param, bias_a, bias_i, gain_one, gain_two)]
    )
    rows = -(-flat.shape[0] // (16 * part)) * 16
    packed = jnp.pad(flat, (0, rows * part - flat.shape[0])).reshape(rows, part)
    first = lax.all_gather(
        jnp.concatenate([w_x.T, w_y.T, packed], axis=0), "seq", axis=1, tiled=True
    )
    second = lax.all_gather(
        jnp.concatenate([w_out, w_gate.T, w_up.T, w_down], axis=0), "seq", axis=1, tiled=True
    )
    if paired:
        firsts, seconds = [first, flip(first, 1)], [second, flip(second, 1)]
    else:
        firsts, seconds = [first], [second]

    def join(arrays, begin, size):
        return jnp.concatenate([a[begin : begin + size] for a in arrays], axis=0)

    wx, wy = join(firsts, 0, channels), join(firsts, channels, channels)
    wo = join(seconds, 0, channels)
    wg = join(seconds, channels, hidden)
    wu = join(seconds, channels + hidden, hidden)
    wd = join(seconds, channels + 2 * hidden, hidden)
    smalls = []
    for a in firsts:
        a = a[2 * channels :].reshape(rows, count, part).transpose(1, 0, 2).reshape(count, -1)
        at, found = 0, []
        for shape in (gate_a.shape, gate_i.shape, conv_w.shape, (thin,), (thin,), (thin,), (part,), (part,)):
            size = 1
            for n in shape:
                size *= n
            found.append(a[:, at : at + size].reshape((count,) + shape))
            at += size
        ga, gi, cw, dp, ba, bi, g1, g2 = found
        ga, gi = (x.transpose(1, 0, 2, 3).reshape(blocks, count * depth, WIDE) for x in (ga, gi))
        cw = cw.transpose(1, 0, 2).reshape(conv_w.shape[0], channels)
        smalls.append((jnp.concatenate([ga, gi], axis=2), cw, dp.reshape(-1), ba.reshape(-1), bi.reshape(-1)))
    gain_1, gain_2 = (g.reshape(-1).astype(jnp.float32) for g in (g1, g2))
    gates = jnp.concatenate([s[0] for s in smalls], axis=0)
    taps = jnp.concatenate([s[1] for s in smalls], axis=1).astype(jnp.float32)
    decay, shift_a, shift_i = (
        jnp.concatenate([s[i] for s in smalls], axis=0).astype(jnp.float32) for i in (2, 3, 4)
    )
    weights = (wx, wy, wo, wg, wu, wd, gates, taps, decay, shift_a, shift_i, gain_1, gain_2)

    if paired:
        core = mp_rank % 2
        mine = lax.dynamic_index_in_dim(tokens, core, 0, keepdims=False)
        other = flip(lax.dynamic_index_in_dim(tokens, 1 - core, 0, keepdims=False), 1)
        stream = jnp.concatenate([mine, other], axis=0).astype(jnp.float32)
        cot = lax.dynamic_index_in_dim(cotangent, core, 0, keepdims=False)
        cot = cot.reshape(SEGS, own_rows, -1)
        cot = jnp.concatenate(
            [lax.dynamic_index_in_dim(cot, s ^ mp_rank, 0, keepdims=False) for s in range(SEGS)],
            axis=0,
        )
        where = jnp.stack([mp_rank, seq_rank]).astype(jnp.int32)
        starts_row = lax.dynamic_index_in_dim(doc_starts, core, 0, keepdims=False)
        block_rows, grad_rows, large, little = micro(
            plan, where, mp_rank, stream, cot, cot[: 2 * own_rows].astype(jnp.float32), starts_row, weights
        )

        def returned(x):
            mine, other = x[:own_rows], flip(x[own_rows:], 1)
            return jnp.where(core == 0, jnp.stack([mine, other]), jnp.stack([other, mine]))

        block_all, grad_all = returned(block_rows), returned(grad_rows)
    else:
        where = jnp.stack([0 * seq_rank, seq_rank]).astype(jnp.int32)
        found = []
        for m in range(micros):
            stream = tokens[m].astype(jnp.float32)
            cot_rows = lax.dynamic_slice_in_dim(cotangent[m], mp_rank * own_rows, own_rows, 0)
            found.append(
                micro(plan, where, 0, stream, cotangent[m], cot_rows.astype(jnp.float32), doc_starts[m], weights)
            )
        block_all = jnp.stack([f[0] for f in found])
        grad_all = jnp.stack([f[1] for f in found])
        large, little = jax.tree.map(lambda *x: sum(x), *[f[2:] for f in found])

    grad_wx, grad_wy, grad_wo, grad_wg, grad_wu, grad_wd = large

    def owned(*grads):
        own = [low(plan.own_sum(g, 0)) for g in grads]
        return lax.psum_scatter(
            jnp.concatenate(own, axis=0), "seq", scatter_dimension=1, tiled=True
        ).astype(jnp.float32)

    late = owned(grad_wx, grad_wy)
    early = owned(grad_wg, grad_wu, grad_wd)
    out_grad = owned(grad_wo)

    grad_gates, lines, gains = little
    if paired:
        grad_gates = grad_gates[:blocks] + flip(grad_gates[blocks:], 1)
        lines = lines[:, :channels] + flip(lines[:, channels:], 1)
    pieces = jnp.concatenate(
        [
            grad_gates.reshape(blocks, count, depth, 2 * WIDE).transpose(1, 0, 2, 3).reshape(count, -1),
            lines.reshape(-1, count, thin).transpose(1, 0, 2).reshape(count, -1),
            gains.reshape(2, count, part).transpose(1, 0, 2).reshape(count, -1),
        ],
        axis=1,
    )
    size = pieces.shape[1]
    pieces = jnp.pad(pieces, ((0, 0), (0, -size % 1024))).reshape(count, -1, WIDE)
    total = lax.dynamic_index_in_dim(pieces, seq_rank, 0, keepdims=False)
    for d in range(1, count):
        piece = lax.dynamic_index_in_dim(pieces, (seq_rank + d) % count, 0, keepdims=False)
        total = total + turned(piece, "seq", d)
    total = total.reshape(-1)
    at = blocks * depth * 2 * WIDE
    sum_gates = total[:at].reshape(blocks, depth, 2, WIDE)
    lines = total[at : at + 7 * thin].reshape(7, thin)
    at += 7 * thin
    gains = total[at : at + 2 * part].reshape(2, part)
    if paired:
        for bits in (1, 2, 4):
            gains = gains + flip(gains, bits)
    else:
        gains = lax.psum(gains, "mp")
    return (
        block_all,
        grad_all,
        late[:channels].T,
        late[channels:].T,
        out_grad,
        early[:hidden].T,
        early[hidden : 2 * hidden].T,
        early[2 * hidden :],
        sum_gates[:, :, 0],
        sum_gates[:, :, 1],
        lines[:4],
        lines[4],
        lines[5],
        lines[6],
        gains[0],
        gains[1],
    )


def solution(mesh):
    return jax.shard_map(
        on_device,
        mesh=mesh,
        in_specs=(
            P(None, ("seq", "mp"), None),
            P(None, "seq", None),
            P("seq", "mp"),
            P("seq", "mp"),
            P("mp", "seq"),
            P("seq", "mp"),
            P("seq", "mp"),
            P("mp", "seq"),
            P("mp", "seq", None),
            P("mp", "seq", None),
            P(None, ("mp", "seq")),
            P(("mp", "seq")),
            P(("mp", "seq")),
            P(("mp", "seq")),
            P("seq"),
            P("seq"),
            P(),
        ),
        out_specs=(
            P(None, ("seq", "mp"), None),
            P(None, ("seq", "mp"), None),
            P("seq", "mp"),
            P("seq", "mp"),
            P("mp", "seq"),
            P("seq", "mp"),
            P("seq", "mp"),
            P("mp", "seq"),
            P("mp", "seq", None),
            P("mp", "seq", None),
            P(None, ("mp", "seq")),
            P(("mp", "seq")),
            P(("mp", "seq")),
            P(("mp", "seq")),
            P("seq"),
            P("seq"),
        ),
        check_vma=False,
    )
```

```python
import functools

import jax
import jax.numpy as jnp
from jax import lax
from jax.experimental import pallas as pl
from jax.experimental.pallas import tpu as pltpu
from jax.sharding import PartitionSpec as P

epsilon = 1e-06
SEGS = 8
WIDE = 128
TILE = 128
ROOT = 0.7978845608028654
CUBE = 0.044715


def gelu_pair(v):
    sq = v * v
    t = jnp.tanh(v * (ROOT + (ROOT * CUBE) * sq))
    half = 0.5 + 0.5 * t
    slope = half + (0.5 * v) * (1.0 - t * t) * (ROOT + (3.0 * CUBE * ROOT) * sq)
    return v * half, slope


def gelu_only(v):
    return v * (0.5 + 0.5 * jnp.tanh(ROOT * v * (1.0 + CUBE * v * v)))


def swapped(x, flips):
    rows = lax.broadcasted_iota(jnp.int32, x.shape, 0)
    for bit in (1, 2, 4):
        down, up = pltpu.roll(x, SEGS - bit, 0), pltpu.roll(x, bit, 0)
        turned = jnp.where((rows & bit) == 0, down, up)
        x = jnp.where((flips & bit) != 0, turned, x)
    return x


def exclusive(prod, last, flips, backward):
    prod, last = swapped(prod, flips), swapped(last, flips)
    one = jnp.ones((1, WIDE), jnp.float32)
    zero = jnp.zeros((1, WIDE), jnp.float32)
    coef, base = [one], [zero]
    order = range(SEGS - 1, -1, -1) if backward else range(SEGS)
    for s in order:
        coef.append(prod[s : s + 1] * coef[-1])
        base.append(prod[s : s + 1] * base[-1] + last[s : s + 1])
    total = jnp.concatenate([coef[-1], base[-1]] + [zero] * (SEGS - 2), axis=0)
    coef, base = coef[:-1], base[:-1]
    if backward:
        coef, base = coef[::-1], base[::-1]
    return (
        swapped(jnp.concatenate(coef, axis=0), flips),
        swapped(jnp.concatenate(base, axis=0), flips),
        total,
    )


def lay_out(blocks, whole):
    size = whole.shape[0] // len(blocks)
    for b, block in enumerate(blocks):
        whole[b * size : (b + 1) * size, :] = block[...]


def enter_kernel(
    parts, where, edge, code, small, gates, *rest
):
    inter, v_out, rg_out, ig_out, e_out, sq_out, maps, total, u = rest[parts:]
    lay_out(rest[:parts], u)
    rows = u.shape[0]
    steps = rows // SEGS
    flips = where[0]

    def lay(s, carry):
        inter[pl.ds(pl.multiple_of(24 + 8 * s, 8), 8), :] = u[pl.ds(s, 8, stride=steps), :]
        return carry

    lax.fori_loop(0, steps, lay, 0, unroll=8)
    first = lax.broadcasted_iota(jnp.int32, (SEGS, WIDE), 0) == 0
    for j in range(3):
        nat = pltpu.roll(swapped(inter[pl.ds(8 * (steps + j), 8), :], flips), 1, 0)
        nat = jnp.where(first, edge[5 + j : 6 + j, :], nat)
        inter[8 * j : 8 * j + 8, :] = swapped(nat, flips)

    def tile(i, carry):
        prod, state = carry
        base = pl.multiple_of(i * TILE, TILE)
        c = code[pl.ds(base, TILE), :]
        v = small[0:1, :] * inter[pl.ds(base + 24, TILE), :]
        for k in (1, 2, 3):
            v = v + jnp.where(
                c >= k, small[k : k + 1, :] * inter[pl.ds(base + 24 - 8 * k, TILE), :], 0.0
            )
        high = v.astype(jnp.bfloat16)
        low = (v - high.astype(jnp.float32)).astype(jnp.bfloat16)
        mat = gates[0]
        pre = jnp.dot(
            jnp.concatenate([high, low], axis=1),
            jnp.concatenate([mat, mat], axis=0),
            preferred_element_type=jnp.float32,
        )
        rg = 1.0 / (1.0 + jnp.exp(-(pre[:, :WIDE] + small[5:6, :])))
        ig = jax.nn.sigmoid(pre[:, WIDE:] + small[6:7, :])
        la = small[4:5, :] * rg
        e = jnp.exp(la)
        sq = jnp.sqrt(jnp.tanh(-la) * (1.0 + e * e))
        here = pl.ds(base, TILE)
        v_out[here, :] = v
        rg_out[here, :] = rg
        ig_out[here, :] = ig
        e_out[here, :] = e
        sq_out[here, :] = sq
        keep = jnp.where(c > 0, e, 0.0)
        inflow = sq * ig * v
        for s in range(TILE // SEGS):
            k = keep[8 * s : 8 * s + 8]
            prod = prod * k
            state = k * state + inflow[8 * s : 8 * s + 8]
        return prod, state

    prod, state = lax.fori_loop(
        0,
        rows // TILE,
        tile,
        (jnp.ones((SEGS, WIDE), jnp.float32), jnp.zeros((SEGS, WIDE), jnp.float32)),
    )
    coef, base, whole = exclusive(prod, state, flips, False)
    maps[0:8, :] = prod
    maps[8:16, :] = coef
    maps[16:24, :] = base
    total[...] = whole


def state_kernel(count, parts, where, v, ig, e, sq, code, maps, *rest):
    others, p_parts = rest[: count - 1], rest[count - 1 : count - 1 + parts]
    hs, out, wide, p = rest[count - 1 + parts :]
    lay_out(p_parts, p)
    rows = v.shape[0]
    steps = rows // SEGS
    mine = where[1]
    entry = jnp.zeros((1, WIDE), jnp.float32)
    for d in range(count - 1, 0, -1):
        piece = others[d - 1]
        entry = jnp.where(mine >= d, piece[0:1, :] * entry + piece[1:2, :], entry)
    state = maps[8:16, :] * entry + maps[16:24, :]
    hs[0:8, :] = state

    def tile(i, state):
        base = pl.multiple_of(i * TILE, TILE)
        here = pl.ds(base, TILE)
        keep = jnp.where(code[here, :] > 0, e[here, :], 0.0)
        inflow = sq[here, :] * ig[here, :] * v[here, :]
        for s in range(TILE // SEGS):
            state = keep[8 * s : 8 * s + 8] * state + inflow[8 * s : 8 * s + 8]
            hs[pl.ds(base + 8 * s + 8, 8), :] = state
            there = pl.ds(i * (TILE // SEGS) + s, 8, stride=steps)
            wide[there, :] = state * gelu_only(p[there, :])
        return state

    lax.fori_loop(0, rows // TILE, tile, state)
    out[...] = wide[...].astype(jnp.bfloat16)


def adjoint_kernel(parts, p_count, where, hs, e, code, maps, *rest):
    dhs, dp, back, total, wide, do, p = rest[parts + p_count :]
    lay_out(rest[:parts], do)
    lay_out(rest[parts : parts + p_count], p)
    rows = do.shape[0]
    steps = rows // SEGS
    flips = where[0]

    def tile(i, grad):
        i = rows // TILE - 1 - i
        base = pl.multiple_of(i * TILE, TILE)
        keep = jnp.where(code[pl.ds(base, TILE), :] > 0, e[pl.ds(base, TILE), :], 0.0)
        for s in range(TILE // SEGS - 1, -1, -1):
            there = pl.ds(i * (TILE // SEGS) + s, 8, stride=steps)
            d = do[there, :]
            act, slope = gelu_pair(p[there, :])
            wide[there, :] = d * hs[pl.ds(base + 8 * s + 8, 8), :] * slope
            dh = d * act
            dhs[pl.ds(base + 8 * s, 8), :] = dh
            grad = keep[8 * s : 8 * s + 8] * (dh + grad)
        return grad

    grad = lax.fori_loop(0, rows // TILE, tile, jnp.zeros((SEGS, WIDE), jnp.float32))
    dp[...] = wide[...].astype(jnp.bfloat16)
    coef, base, whole = exclusive(maps[0:8, :], grad, flips, True)
    back[0:8, :] = coef
    back[8:16, :] = base
    total[...] = whole


def leave_kernel(count, where, dhs, inter, v, rg, ig, e, sq, hs, code, small, gates_t, back, *rest):
    products, grads = rest[: count - 1], rest[count - 1 : 2 * count - 2]
    du, grad_gates, sums, edge, dv_all, wide = rest[2 * count - 1 :]
    rows = dhs.shape[0]
    steps = rows // SEGS
    flips, mine = where[0], where[1]
    entry = jnp.zeros((1, WIDE), jnp.float32)
    for j in range(count - 1, 0, -1):
        d = count - j
        entry = jnp.where(
            mine + j < count, products[d - 1][0:1, :] * entry + grads[d - 1][1:2, :], entry
        )
    grad = back[0:8, :] * entry + back[8:16, :]
    grad_gates[...] = jnp.zeros_like(grad_gates)

    def fold(x):
        parts = [x[8 * s : 8 * s + 8] for s in range(TILE // SEGS)]
        while len(parts) > 1:
            parts = [a + b for a, b in zip(parts[::2], parts[1::2])]
        return parts[0]

    def tile(i, carry):
        grad, taps, decay, shift_a, shift_i = carry
        i = rows // TILE - 1 - i
        base = pl.multiple_of(i * TILE, TILE)
        here = pl.ds(base, TILE)
        c = code[here, :]
        e_now, sq_now, rg_now, ig_now, v_now = e[here, :], sq[here, :], rg[here, :], ig[here, :], v[here, :]
        keep = jnp.where(c > 0, e_now, 0.0)
        d_now = dhs[here, :]
        pieces = [None] * (TILE // SEGS)
        for s in range(TILE // SEGS - 1, -1, -1):
            a = d_now[8 * s : 8 * s + 8] + grad
            pieces[s] = a
            grad = keep[8 * s : 8 * s + 8] * a
        a = jnp.concatenate(pieces, axis=0)
        q = ig_now * v_now
        dla = a * (keep * hs[here, :] - q * (e_now * e_now) / jnp.maximum(sq_now, 1e-25))
        rate = rg_now * dla
        decay = decay + fold(rate)
        dra = small[4:5, :] * rate * (1.0 - rg_now)
        asq = a * sq_now
        dia = asq * q * (1.0 - ig_now)
        shift_a = shift_a + fold(dra)
        shift_i = shift_i + fold(dia)
        both = jnp.concatenate([dra.astype(jnp.bfloat16), dia.astype(jnp.bfloat16)], axis=1)
        dv = asq * ig_now + jnp.dot(both, gates_t[0], preferred_element_type=jnp.float32)
        grad_gates[0] += lax.dot_general(
            v_now.astype(jnp.bfloat16),
            both,
            (((0,), (0,)), ((), ())),
            preferred_element_type=jnp.float32,
        )
        dv_all[here, :] = dv
        new_taps = [taps[0] + fold(dv * inter[pl.ds(base + 24, TILE), :])]
        for k in (1, 2, 3):
            new_taps.append(
                taps[k]
                + fold(jnp.where(c >= k, dv * inter[pl.ds(base + 24 - 8 * k, TILE), :], 0.0))
            )
        return grad, tuple(new_taps), decay, shift_a, shift_i

    zero = jnp.zeros((SEGS, WIDE), jnp.float32)
    _, taps, decay, shift_a, shift_i = lax.fori_loop(
        0, rows // TILE, tile, (grad, (zero,) * 4, zero, zero, zero)
    )
    totals = [jnp.sum(x, axis=0, keepdims=True) for x in (*taps, decay, shift_a, shift_i)]
    sums[...] = jnp.concatenate(totals + [jnp.zeros((1, WIDE), jnp.float32)], axis=0)
    last = lax.broadcasted_iota(jnp.int32, (SEGS, WIDE), 0) == SEGS - 1
    edges = []
    for j in range(3):
        nat = swapped(dv_all[8 * j : 8 * j + 8, :], flips)
        edges.append(nat[0:1])
        nat = jnp.where(last, 0.0, pltpu.roll(nat, SEGS - 1, 0))
        dv_all[pl.ds(rows + 8 * j, 8), :] = swapped(nat, flips)
    edge[...] = jnp.concatenate(edges + [jnp.zeros((SEGS - 3, WIDE), jnp.float32)], axis=0)

    def mix(i, carry):
        base = pl.multiple_of(i * TILE, TILE)
        total = small[0:1, :] * dv_all[pl.ds(base, TILE), :]
        for k in (1, 2, 3):
            there = pl.ds(base + 8 * k, TILE)
            total = total + jnp.where(
                code[there, :] >= k, small[k : k + 1, :] * dv_all[there, :], 0.0
            )
        for s in range(TILE // SEGS):
            wide[pl.ds(i * (TILE // SEGS) + s, 8, stride=steps), :] = total[8 * s : 8 * s + 8]
        return carry

    lax.fori_loop(0, rows // TILE, mix, 0)
    du[...] = wide[...].astype(jnp.bfloat16)


def copy_kernel(pick, x, out):
    out[...] = x[0, 0]


def reordered(pick, x, name):
    _, segs, rows, width = x.shape
    return pl.pallas_call(
        copy_kernel,
        grid_spec=pltpu.PrefetchScalarGridSpec(
            num_scalar_prefetch=1,
            grid=(segs,),
            in_specs=[pl.BlockSpec((1, 1, rows, width), lambda s, p: (p[1], s ^ p[0], 0, 0))],
            out_specs=pl.BlockSpec((rows, width), lambda s, p: (s, 0)),
        ),
        out_shape=jax.ShapeDtypeStruct((segs * rows, width), x.dtype),
        cost_estimate=cost(0.3),
        name=name,
    )(pick, x)


def nt(left_mat, right_mat):
    return lax.dot_general(
        left_mat, right_mat, (((1,), (1,)), ((), ())), preferred_element_type=jnp.float32
    )


def cost(us):
    return pl.CostEstimate(flops=int(us * 1e9), bytes_accessed=1, transcendentals=0)


def nt(left_mat, right_mat):
    return lax.dot_general(
        left_mat, right_mat, (((1,), (1,)), ((), ())), preferred_element_type=jnp.float32
    )


def mlp_kernel(h, dy, wg, wu, wd, mid, low_gate, low_up, part):
    up_pre = nt(h[...], wu[...])
    act, slope = gelu_pair(nt(h[...], wg[...]))
    grad_mid = nt(dy[...], wd[...])
    mid[...] = (act * up_pre).astype(jnp.bfloat16)
    low_gate[...] = (grad_mid * (up_pre * slope)).astype(jnp.bfloat16)
    low_up[...] = (grad_mid * act).astype(jnp.bfloat16)
    part[...] = (
        jnp.dot(low_gate[...], wg[...], preferred_element_type=jnp.float32)
        + jnp.dot(low_up[...], wu[...], preferred_element_type=jnp.float32)
    ).astype(part.dtype)


def mlp(h, cot, block, wg, wu, wd, kind):
    rows, width = h.shape
    hidden = wg.shape[0]
    step = min(rows, 256)
    count = rows // step
    row_spec = pl.BlockSpec((step, width), lambda j: (j, 0))
    cot_spec = pl.BlockSpec((step, width), lambda j: (j + block * count, 0))
    weight = pl.BlockSpec((hidden, width), lambda j: (0, 0))
    act = pl.BlockSpec((step, hidden), lambda j: (j, 0))
    low_shape = jax.ShapeDtypeStruct((rows, hidden), jnp.bfloat16)
    wg, wu, wd = (pltpu.with_memory_space_constraint(w, pltpu.VMEM) for w in (wg, wu, wd))
    return pl.pallas_call(
        mlp_kernel,
        grid=(count,),
        in_specs=[row_spec, cot_spec, weight, weight, weight],
        out_specs=[act, act, act, row_spec],
        out_shape=[low_shape] * 3 + [jax.ShapeDtypeStruct((rows, width), kind)],
        compiler_params=pltpu.CompilerParams(vmem_limit_bytes=24 * 2**20),
        cost_estimate=cost(0.3),
        name="mlp",
    )(h, cot, wg, wu, wd)


CHUNK = 96


def grads_kernel(spans, lefts, which, cuts, added, *refs):
    rights = [refs[lefts + i] for i in which]
    more = refs[lefts + max(which) + 1 :][:added]
    outs = refs[lefts + max(which) + 1 + added :]
    count, _, part = outs[0].shape
    at = 0
    for left, right, (low_col, high_col) in zip(refs[:lefts], rights, spans):
        first = low_col // WIDE * WIDE
        last = min(-(-high_col // WIDE) * WIDE, left.shape[1])
        total = lax.dot_general(
            left[:, first:last],
            right[...],
            (((0,), (0,)), ((), ())),
            preferred_element_type=jnp.float32,
        )
        done = 0
        while done < high_col - low_col:
            size = min(cuts, high_col - low_col - done)
            rows = low_col - first + done
            for z in range(count):
                piece = total[rows : rows + size, z * part : (z + 1) * part]
                if added:
                    piece = piece + more[at // cuts][z].astype(jnp.float32)
                if len(outs) > 1:
                    outs[at // cuts][z] = piece.astype(jnp.bfloat16)
                else:
                    outs[0][z, at : at + size, :] = piece.astype(jnp.bfloat16)
            done += size
            at += size


def grads(pairs, half, halves, count, split=False, added=()):
    spans, rows = [], 0
    for left, _ in pairs:
        size = left.shape[1] // halves
        spans.append((half * size, (half + 1) * size))
        rows += size
    part = pairs[0][1].shape[1] // count
    sizes = [b - a for a, b in spans]
    cuts = rows if len(sizes) == 1 else 16
    if split or added:
        cuts = next(c for c in (CHUNK, 64, 16) if all(s % c == 0 for s in sizes))
    rights, which = [], []
    for _, right in pairs:
        if not any(right is r for r in rights):
            rights.append(right)
        which.append(next(i for i, r in enumerate(rights) if r is right))
    args = [p[0] for p in pairs] + rights + list(added)
    shape = (count, cuts if split else rows, part)
    return pl.pallas_call(
        functools.partial(grads_kernel, spans, len(pairs), which, cuts, len(added)),
        out_shape=[jax.ShapeDtypeStruct(shape, jnp.bfloat16)] * (rows // cuts if split else 1),
        compiler_params=pltpu.CompilerParams(vmem_limit_bytes=32 * 2**20),
        cost_estimate=cost(0.3),
        name="grads",
    )(*args)


def lanes(rows, offset=0):
    return pl.BlockSpec((rows, WIDE), lambda n: (0, n + offset))


def paths(rows, groups, halves, offset):
    size = groups // halves
    return pl.BlockSpec((rows, WIDE), lambda n: (0, n + (n // size + offset) * size))


def per_block(shape):
    return pl.BlockSpec((1,) + shape, lambda n: (n, 0, 0))


def scalars():
    return pl.BlockSpec(memory_space=pltpu.SMEM)


def shared(shape):
    return pl.BlockSpec(shape, lambda n: (0,) * len(shape))


def launch(kernel, groups, in_specs, outs, scratch, args, name, aliases={}):
    def place(shape, dtype):
        if shape[0] >= 512 and dtype == jnp.float32:
            return pltpu.HBM(shape, dtype)
        return jax.ShapeDtypeStruct(shape, dtype)

    def pin(a):
        if a.shape[0] >= 512 and a.dtype == jnp.float32 and a.shape[1] > WIDE:
            return pltpu.with_memory_space_constraint(a, pltpu.HBM)
        return a

    return pl.pallas_call(
        kernel,
        grid=(groups,),
        in_specs=in_specs,
        out_specs=[spec for _, _, spec in outs],
        out_shape=[place(shape, dtype) for shape, dtype, _ in outs],
        scratch_shapes=scratch,
        compiler_params=pltpu.CompilerParams(vmem_limit_bytes=16 * 2**20),
        cost_estimate=cost(0.3),
        name=name,
        input_output_aliases=aliases,
    )(*[pin(a) for a in args])


def enter(where, both, edge, code, small, gates, halves):
    parts, size = len(both), both[0].shape[0]
    rows, channels = parts * size, both[0].shape[1] // 2
    groups = channels // WIDE
    f32 = jnp.float32
    full = ((rows, channels), f32, lanes(rows))
    return launch(
        functools.partial(enter_kernel, parts),
        groups,
        [
            scalars(),
            paths(8, groups, halves, 0),
            shared(code.shape),
            lanes(8),
            per_block((WIDE, 2 * WIDE)),
        ]
        + [paths(size, groups, halves, 0)] * parts,
        [
            ((rows + 24, channels), f32, lanes(rows + 24)),
            full,
            full,
            full,
            full,
            full,
            ((24, channels), f32, lanes(24)),
            ((8, channels), f32, lanes(8)),
        ],
        [pltpu.VMEM((rows, WIDE), f32)],
        (where, edge, code, small, gates, *both),
        "enter",
    )


def states_of(where, v, ig, e, sq, code, both, maps, others, halves):
    rows, channels = v.shape
    parts, size = len(both), both[0].shape[0]
    groups = channels // WIDE
    f32 = jnp.float32
    return launch(
        functools.partial(state_kernel, len(others) + 1, parts),
        groups,
        [scalars()]
        + [lanes(rows)] * 4
        + [shared(code.shape), lanes(24)]
        + [lanes(8)] * len(others)
        + [paths(size, groups, halves, 1)] * parts,
        [
            ((rows + 8, channels), f32, lanes(rows + 8)),
            ((rows, channels), jnp.bfloat16, lanes(rows)),
        ],
        [pltpu.VMEM((rows, WIDE), f32)] * 2,
        (where, v, ig, e, sq, code, maps, *others, *both),
        "states",
    )


def adjoints(where, do, both, hs, e, code, maps, halves):
    parts, (size, channels) = len(do), do[0].shape
    p_count, p_size = len(both), both[0].shape[0]
    rows = parts * size
    groups = channels // WIDE
    f32 = jnp.float32
    return launch(
        functools.partial(adjoint_kernel, parts, p_count),
        groups,
        [scalars(), lanes(rows + 8), lanes(rows), shared(code.shape), lanes(24)]
        + [lanes(size)] * parts
        + [paths(p_size, groups, halves, 1)] * p_count,
        [
            ((rows, channels), f32, lanes(rows)),
            ((rows, 2 * channels), jnp.bfloat16, paths(rows, groups, halves, 1)),
            ((16, channels), f32, lanes(16)),
            ((8, channels), f32, lanes(8)),
        ],
        [pltpu.VMEM((rows, WIDE), f32)] * 3,
        (where, hs, e, code, maps, *do, *both),
        "adjoint",
    )


def leave(where, dhs, kept, hs, code, small, gates_t, back, products, grads, half_done, halves):
    inter, v, rg, ig, e, sq = kept
    rows, channels = dhs.shape
    groups = channels // WIDE
    f32 = jnp.float32
    count = len(products) + 1
    return launch(
        functools.partial(leave_kernel, count),
        groups,
        [scalars(), lanes(rows), lanes(rows + 24)]
        + [lanes(rows)] * 5
        + [
            lanes(rows + 8),
            shared(code.shape),
            lanes(8),
            per_block((2 * WIDE, WIDE)),
            lanes(16),
        ]
        + [lanes(8)] * (2 * count - 2)
        + [pl.BlockSpec(memory_space=pl.ANY)],
        [
            ((rows, 2 * channels), jnp.bfloat16, paths(rows, groups, halves, 0)),
            ((groups, WIDE, 2 * WIDE), f32, per_block((WIDE, 2 * WIDE))),
            ((8, channels), f32, lanes(8)),
            ((8, channels), f32, lanes(8)),
        ],
        [pltpu.VMEM((rows + 24, WIDE), f32), pltpu.VMEM((rows, WIDE), f32)],
        (where, dhs, inter, v, rg, ig, e, sq, hs, code, small, gates_t, back, *products, *grads, half_done),
        "leave",
        {11 + 2 * count: 0},
    )


def dense(left_mat, right_mat):
    return jnp.dot(left_mat, right_mat, preferred_element_type=jnp.float32)


def dense_nt(left_mat, right_mat):
    return lax.dot_general(
        left_mat, right_mat, (((1,), (1,)), ((), ())), preferred_element_type=jnp.float32
    )


def dense_tn(left_mat, right_mat):
    return lax.dot_general(
        left_mat, right_mat, (((0,), (0,)), ((), ())), preferred_element_type=jnp.float32
    )


def low(x):
    return x.astype(jnp.bfloat16)


def high(x):
    return x.astype(jnp.float32)


def after(x, *others):
    return lax.optimization_barrier((x,) + others)[0]


def tied(*values):
    return lax.optimization_barrier(values)


def turned(x, axis, distance):
    count = lax.axis_size(axis)
    return lax.ppermute(x, axis, [(i, (i + distance) % count) for i in range(count)])


def around(x, axis):
    return [turned(x, axis, d) for d in range(1, lax.axis_size(axis))]


def in_order(x, pieces, axis):
    count = lax.axis_size(axis)
    mine = lax.axis_index(axis)
    turn = jnp.stack([x] + pieces[::-1])
    turn = jnp.concatenate([turn, turn], axis=0)
    return lax.dynamic_slice_in_dim(turn, (count - mine) % count, count, 0)


def flip(x, bits):
    count = lax.axis_size("mp")
    return lax.ppermute(x, "mp", [(i, i ^ bits) for i in range(count)])


class Paired:
    halves = 2
    blocks = 4

    def spread(self, rows):
        half = rows.shape[0] // 2
        a, b = rows[:half], rows[half:]
        xb, ya = flip(b, 2), flip(a, 4)
        xa, yb = flip(a, 2), flip(b, 4)
        da, db = flip(ya, 2), flip(xb, 4)
        pairs = ((xa, xb), (ya, yb), (da, db))
        return [rows] + [jnp.concatenate(p, axis=0) for p in pairs], (da, db)

    def give(self, part, block):
        return part if block == 0 else flip(part, 2 * block)

    def gather_sum(self, pieces):
        total = high(pieces[0])
        for piece in pieces[1:]:
            total = total + high(piece)
        return total

    def collect(self, part):
        p3 = low(part(3))
        half = p3.shape[0] // 2
        r2a, r1b = flip(p3[:half], 2), flip(p3[half:], 4)
        p1, p2 = part(1), part(2)
        s1a, s2b = flip(low(p1[:half]), 2), flip(low(p2[half:]), 4)
        p0 = part(0)
        s2a = flip(low(high(p2[:half]) + high(r2a)), 4)
        s1b = flip(low(high(p1[half:]) + high(r1b)), 2)
        return (p0, s1a, s1b, s2a, s2b), (r2a, r1b)

    def finish(self, pieces):
        p0, s1a, s1b, s2a, s2b = pieces
        far = [
            jnp.concatenate([s1a, s1b], axis=0),
            jnp.concatenate([s2a, s2b], axis=0),
        ]
        return high(p0) + high(far[0]) + high(far[1])

    def both(self, x):
        return [x, flip(x, 1)]

    def sent_totals(self, pairs, count):
        return [flip(x, 1) for x in grads(pairs, 1, 2, count, split=True)]

    def own_totals(self, pairs, count, sent):
        return grads(pairs, 0, 2, count, added=sent)[0]


class Plain:
    halves = 1
    blocks = 1

    def spread(self, rows):
        rows = lax.all_gather(rows, "mp", axis=0, tiled=True)
        return [rows], (rows,)

    def collect(self, part):
        rows = lax.psum_scatter(low(part(0)), "mp", scatter_dimension=0, tiled=True)
        return (rows,), (rows,)

    def finish(self, pieces):
        return high(pieces[0])

    def both(self, x):
        return [x]

    def sent_totals(self, pairs, count):
        return []

    def own_totals(self, pairs, count, sent):
        return grads(pairs, 0, 1, count)[0]


def mask_code(starts_row, first_pos, flips, steps):
    shape = ((steps + 3) * SEGS, WIDE)
    row = lax.broadcasted_iota(jnp.int32, shape, 0)
    places = first_pos + ((row & (SEGS - 1)) ^ flips) * steps + (row // SEGS)
    code = jnp.full(shape, 4, jnp.int32)
    for e in range(starts_row.shape[0]):
        away = places - starts_row[e]
        code = jnp.where((starts_row[e] > 0) & (away >= 0), jnp.minimum(code, away), code)
    return code.astype(jnp.float32)


def normed(rows):
    scale = lax.rsqrt(jnp.mean(rows * rows, axis=-1, keepdims=True) + epsilon)
    return rows * scale, scale


def norm_back(grad_norm, norm, scale):
    return scale * (grad_norm - norm * jnp.mean(grad_norm * norm, axis=-1, keepdims=True))


def small_weights(gate_a, gate_i, conv_w, decay_param, bias_a, bias_i, gain_one, gain_two):
    blocks, depth, _ = gate_a.shape
    taps, thin = conv_w.shape
    part = gain_one.shape[0]
    count = lax.axis_size("seq")
    if part % WIDE == 0 and thin <= WIDE:
        lines = jnp.concatenate([conv_w, decay_param[None], bias_a[None], bias_i[None]], axis=0)
        lines = jnp.pad(lines, ((0, 1), (0, WIDE - thin)))
        gains = jnp.concatenate([gain_one.reshape(-1, WIDE), gain_two.reshape(-1, WIDE)], axis=0)
        pack = jnp.concatenate(
            [gate_a.reshape(-1, WIDE), gate_i.reshape(-1, WIDE), lines, gains], axis=0
        )
        pack = jnp.pad(pack, ((0, -pack.shape[0] % 16), (0, 0)))
        pack = in_order(pack, around(pack, "seq"), "seq")
        at = blocks * depth
        ga, gi = (
            pack[:, i * at : (i + 1) * at].reshape(count, blocks, depth, WIDE).transpose(1, 0, 2, 3)
            for i in (0, 1)
        )
        ga, gi = (x.reshape(blocks, count * depth, WIDE) for x in (ga, gi))
        lines = pack[:, 2 * at : 2 * at + taps + 3, :thin].transpose(1, 0, 2).reshape(taps + 3, -1)
        at = 2 * at + taps + 4
        size = part // WIDE
        gain_one = pack[:, at : at + size].reshape(-1)
        gain_two = pack[:, at + size : at + 2 * size].reshape(-1)
    else:
        ga, gi = (lax.all_gather(x, "seq", axis=1, tiled=True) for x in (gate_a, gate_i))
        lines = jnp.concatenate([conv_w, decay_param[None], bias_a[None], bias_i[None]], axis=0)
        lines = lax.all_gather(lines, "seq", axis=1, tiled=True)
        gain_one, gain_two = (
            lax.all_gather(x, "seq", axis=0, tiled=True) for x in (gain_one, gain_two)
        )
    return jnp.concatenate([ga, gi], axis=2), high(lines), high(gain_one), high(gain_two)


def micro(plan, where, flips, stream, cot, starts_row, weights):
    first, second, smalls = weights
    count = stream.shape[0] * lax.axis_size("mp") // plan.halves
    steps = count // SEGS
    size = count // plan.blocks
    blocks_of_z = lax.axis_size("seq")
    seq_rank = lax.axis_index("seq")
    wide = plan.halves
    def rows_of(x, b):
        return x[b * size : (b + 1) * size]

    n1, s1 = normed(stream)
    low_n1 = low(n1)
    h1, _ = plan.spread(low_n1)
    come = h1[min(1, plan.blocks - 1)]
    starts_row = after(starts_row, come)
    code = mask_code(starts_row, seq_rank * count, flips, steps)
    gates, lines, gain_one, gain_two = small_weights(*after(smalls, come))
    gates = jnp.concatenate(plan.both(gates), axis=0)
    lines = jnp.concatenate(plan.both(lines), axis=1)
    taps, decay = lines[:4], lines[4]
    channels = lines.shape[1]
    own = channels // wide
    rate = -8.0 * jax.nn.softplus(decay)
    small = jnp.concatenate([taps, rate[None], lines[5:7], jnp.zeros((1, channels))], axis=0)
    gates_t = jnp.concatenate(
        [gates[:, :, :WIDE].transpose(0, 2, 1), gates[:, :, WIDE:].transpose(0, 2, 1)], axis=1
    )
    h1 = jnp.concatenate([low(high(h) * gain_one) for h in h1], axis=0)
    other = plan.both(after(first, h1, code, small, gates, gates_t))
    wxy = jnp.concatenate([x[i] for x in other for i in (0, 1)], axis=0)
    wo = jnp.concatenate([x[2] for x in other], axis=0)
    up_both = [dense_nt(rows_of(h1, b), wxy) for b in range(plan.blocks)]
    last = lax.dynamic_slice_in_dim(h1, ((SEGS - 1) ^ flips) * steps + steps - 8, 8, 0)
    before = turned(last, "seq", 1)
    edge = jnp.where(seq_rank > 0, dense_nt(before, wxy), 0.0)
    *kept, maps, total = enter(where, up_both, edge, code, small, gates, wide)
    inter, v, rg, ig, e, sq = kept
    fore = around(total, "seq")
    hs, mixed = states_of(where, v, ig, e, sq, code, up_both, maps, fore, wide)

    more, come = plan.collect(lambda b: dense(rows_of(mixed, b), wo))
    cot = cot(come[0])
    middle = stream + plan.finish(after(more, cot))
    n2, s2 = normed(middle)
    h2, come = plan.spread(low(n2 * gain_two))
    second = after(second, *come)
    third = second.shape[0] // 3
    wg, wu, wd = (
        jnp.concatenate(plan.both(second[i * third : (i + 1) * third]), axis=0) for i in range(3)
    )
    each = range(plan.blocks)
    found = {}
    for b in list(each)[::-1]:
        kind = jnp.float32 if b == 0 and plan.blocks > 1 else jnp.bfloat16
        found[b] = mlp(h2[b], cot, b, wg, wu, wd, kind)
    back_two, come = plan.collect(lambda b: found[b][3])
    mid, low_gate, low_up = (
        jnp.concatenate([found[b][i] for b in each], axis=0) for i in (0, 1, 2)
    )
    h2 = jnp.concatenate(h2, axis=0)
    mid = after(mid, *come)
    low_gate = after(low_gate, *back_two[1:])
    sent_wd = plan.sent_totals([(mid, cot)], blocks_of_z)
    pack_wd = plan.own_totals([(mid, cot)], blocks_of_z, sent_wd)
    grad_wd = owner_sum(pack_wd)
    pairs = [(low_gate, h2), (low_up, h2)]
    pack_gate_up = plan.own_totals(pairs, blocks_of_z, plan.sent_totals(pairs, blocks_of_z))
    grad_gate_up = owner_sum(pack_gate_up)
    back_two = plan.finish(after(back_two, pack_wd, pack_gate_up))
    grad_two = jnp.sum(back_two * n2, axis=0)
    grad_middle = high(cot_rows_of(plan, cot, stream.shape[0])) + norm_back(
        back_two * gain_two, n2, s2
    )
    low_middle = low(grad_middle)
    mid_rows, _ = plan.spread(low_middle)
    shares = dense(after(mid, low_middle), wd)
    shares = [rows_of(shares, b) for b in each]
    shares = [x if b == 0 else low(x) for b, x in enumerate(shares)]
    mid_rows = after(jnp.concatenate(mid_rows, axis=0), *shares)
    do = [dense_nt(mid_rows, wo)]
    block_parts, _ = plan.collect(lambda b: after(shares[b], do[0]))
    dhs, dup, back, total = adjoints(where, do, up_both, hs, e, code, maps, wide)
    aft = around(total, "seq")
    dhs, grad_wd = tied(dhs, grad_wd)
    dup, grad_gates, sums, edge = leave(
        where, dhs, kept, hs, code, small, gates_t, back, fore, aft, dup, wide
    )
    nxt = jnp.where(seq_rank < lax.axis_size("seq") - 1, turned(edge, "seq", -1), 0.0)
    spots = [(steps + j) * SEGS + ((SEGS - 1) ^ flips) for j in range(3)]
    far = jnp.concatenate([lax.dynamic_slice(code, (i, 0), (1, 1)) for i in spots], axis=0)
    extra = [jnp.zeros((5, channels))]
    for j in range(3):
        row = jnp.zeros((1, channels))
        for k in range(3 - j, 4):
            i = j + k - 3
            row = row + jnp.where(far[i : i + 1] >= k, taps[k : k + 1] * nxt[i : i + 1], 0.0)
        extra.append(row)
    extra = jnp.concatenate(extra, axis=0)
    at = ((SEGS - 1) ^ flips) * steps + steps - 8
    extra = low(interleaved(extra, jnp.zeros_like(extra), wide))
    patch = low(high(lax.dynamic_slice_in_dim(dup, at, 8, 0)) + high(extra))
    dup = lax.dynamic_update_slice_in_dim(dup, patch, at, 0)
    pairs = [(dup, h1), (mixed, mid_rows)]
    pack_late = plan.own_totals(pairs, blocks_of_z, plan.sent_totals(pairs, blocks_of_z))
    dup, pack_late = tied(dup, pack_late)
    parts = {b: dense(rows_of(dup, b), wxy) for b in list(each)[::-1]}
    back_one, _ = plan.collect(lambda b: parts[b])
    block_rows = low(middle + plan.finish(after(block_parts, parts[0])))
    grad_one = sum(jnp.sum(parts[b] * high(rows_of(h1, b)), axis=0) for b in parts) / gain_one
    pack_late, grad_gate_up = tied(pack_late, grad_gate_up)
    late = owner_sum(pack_late)
    back_one = plan.finish(back_one)
    grad_rows = low(grad_middle + norm_back(back_one * gain_one, n1, s1))
    decay_sum = -8.0 * jax.nn.sigmoid(decay) * sums[4]
    sums = jnp.concatenate([sums[:4], decay_sum[None], sums[5:7]], axis=0)
    little = (grad_gates, sums, jnp.stack([grad_one, grad_two]))
    large = tuple(high(x) for x in (late, grad_gate_up, grad_wd))
    return block_rows, grad_rows, large, little


def interleaved(first, second, halves):
    size = first.shape[1] // halves
    return jnp.concatenate(
        [x[:, i * size : (i + 1) * size] for i in range(halves) for x in (first, second)], axis=1
    )


def cot_rows_of(plan, cot, rows):
    if plan.halves == 2:
        return cot[:rows]
    return lax.dynamic_slice_in_dim(cot, lax.axis_index("mp") * rows, rows, 0)


def owner_sum(pack):
    return lax.psum_scatter(pack, "seq", scatter_dimension=0, tiled=False)


def on_device(
    tokens,
    cotangent,
    w_x,
    w_y,
    w_out,
    w_gate,
    w_up,
    w_down,
    gate_a,
    gate_i,
    conv_w,
    decay_param,
    bias_a,
    bias_i,
    gain_one,
    gain_two,
    doc_starts,
):
    micros, own_rows, _ = tokens.shape
    span = cotangent.shape[1]
    count = lax.axis_size("seq")
    seq_rank = lax.axis_index("seq")
    mp_rank = lax.axis_index("mp")
    paired = micros == 2 and lax.axis_size("mp") == SEGS and span == SEGS * own_rows
    plan = Paired() if paired else Plain()
    channels, hidden = w_x.shape[1], w_gate.shape[1]
    blocks, depth, _ = gate_a.shape
    part = w_x.shape[0]
    thin = conv_w.shape[1]

    first = lax.all_gather(
        jnp.stack([w_x.T, w_y.T, w_out]), "seq", axis=2, tiled=True
    )
    second = lax.all_gather(
        jnp.concatenate([w_gate.T, w_up.T, w_down], axis=0), "seq", axis=1, tiled=True
    )
    smalls = (gate_a, gate_i, conv_w, decay_param, bias_a, bias_i, gain_one, gain_two)
    weights = (first, second, smalls)

    if paired:
        core = mp_rank % 2
        mine = lax.dynamic_index_in_dim(tokens, core, 0, keepdims=False)
        other = flip(lax.dynamic_index_in_dim(tokens, 1 - core, 0, keepdims=False), 1)
        stream = high(jnp.concatenate([mine, other], axis=0))
        pick = jnp.stack([mp_rank, core]).astype(jnp.int32)
        folded = cotangent.reshape(micros, SEGS, own_rows, -1)
        where = jnp.stack([mp_rank, seq_rank]).astype(jnp.int32)
        starts_row = lax.dynamic_index_in_dim(doc_starts, core, 0, keepdims=False)
        block_rows, grad_rows, large, little = micro(
            plan,
            where,
            mp_rank,
            stream,
            lambda come: reordered(after(pick, come), folded, "order"),
            starts_row,
            weights,
        )

        def returned(x):
            mine, other = x[:own_rows], flip(x[own_rows:], 1)
            return jnp.where(core == 0, jnp.stack([mine, other]), jnp.stack([other, mine]))

        block_all, grad_all = returned(block_rows), returned(grad_rows)
    else:
        where = jnp.stack([0 * seq_rank, seq_rank]).astype(jnp.int32)
        found = [
            micro(plan, where, 0, high(tokens[m]), lambda come, m=m: cotangent[m], doc_starts[m], weights)
            for m in range(micros)
        ]
        block_all = jnp.stack([f[0] for f in found])
        grad_all = jnp.stack([f[1] for f in found])
        large, little = jax.tree.map(lambda *x: sum(x), *[f[2:] for f in found])

    late, gate_up_grad, down_grad = large
    grad_gates, lines, gains = little
    if paired:
        grad_gates = grad_gates[:blocks] + flip(grad_gates[blocks:], 1)
        lines = lines[:, :channels] + flip(lines[:, channels:], 1)
    pieces = jnp.concatenate(
        [
            grad_gates.reshape(blocks, count, depth, 2 * WIDE).transpose(1, 0, 2, 3).reshape(count, -1),
            lines.reshape(-1, count, thin).transpose(1, 0, 2).reshape(count, -1),
            gains.reshape(2, count, part).transpose(1, 0, 2).reshape(count, -1),
        ],
        axis=1,
    )
    size = pieces.shape[1]
    pieces = jnp.pad(pieces, ((0, 0), (0, -size % 1024))).reshape(count, -1, WIDE)
    total = lax.dynamic_index_in_dim(pieces, seq_rank, 0, keepdims=False)
    for d in range(1, count):
        piece = lax.dynamic_index_in_dim(pieces, (seq_rank + d) % count, 0, keepdims=False)
        total = total + turned(piece, "seq", d)
    total = total.reshape(-1)
    at = blocks * depth * 2 * WIDE
    sum_gates = total[:at].reshape(blocks, depth, 2, WIDE)
    lines = total[at : at + 7 * thin].reshape(7, thin)
    at += 7 * thin
    gains = total[at : at + 2 * part].reshape(2, part)
    if paired:
        gains = after(gains, grad_rows)
        for bits in (1, 2, 4):
            gains = gains + flip(gains, bits)
    else:
        gains = lax.psum(gains, "mp")
    return (
        block_all,
        grad_all,
        late[:channels].T,
        late[channels : 2 * channels].T,
        late[2 * channels :],
        gate_up_grad[:hidden].T,
        gate_up_grad[hidden:].T,
        down_grad,
        sum_gates[:, :, 0],
        sum_gates[:, :, 1],
        lines[:4],
        lines[4],
        lines[5],
        lines[6],
        gains[0],
        gains[1],
    )


def solution(mesh):
    return jax.shard_map(
        on_device,
        mesh=mesh,
        in_specs=(
            P(None, ("seq", "mp"), None),
            P(None, "seq", None),
            P("seq", "mp"),
            P("seq", "mp"),
            P("mp", "seq"),
            P("seq", "mp"),
            P("seq", "mp"),
            P("mp", "seq"),
            P("mp", "seq", None),
            P("mp", "seq", None),
            P(None, ("mp", "seq")),
            P(("mp", "seq")),
            P(("mp", "seq")),
            P(("mp", "seq")),
            P("seq"),
            P("seq"),
            P(),
        ),
        out_specs=(
            P(None, ("seq", "mp"), None),
            P(None, ("seq", "mp"), None),
            P("seq", "mp"),
            P("seq", "mp"),
            P("mp", "seq"),
            P("seq", "mp"),
            P("seq", "mp"),
            P("mp", "seq"),
            P("mp", "seq", None),
            P("mp", "seq", None),
            P(None, ("mp", "seq")),
            P(("mp", "seq")),
            P(("mp", "seq")),
            P(("mp", "seq")),
            P("seq"),
            P("seq"),
        ),
        check_vma=False,
    )
```

```python
import functools

import jax
import jax.numpy as jnp
from jax import lax
from jax.experimental import pallas as pl
from jax.experimental.pallas import tpu as pltpu
from jax.sharding import PartitionSpec as P

epsilon = 1e-06
SEGS = 8
WIDE = 128
TILE = 128
ROOT = 0.7978845608028654
CUBE = 0.044715


def gelu_pair(v):
    sq = v * v
    t = jnp.tanh(v * (ROOT + (ROOT * CUBE) * sq))
    half = 0.5 + 0.5 * t
    slope = half + (0.5 * v) * (1.0 - t * t) * (ROOT + (3.0 * CUBE * ROOT) * sq)
    return v * half, slope


def gelu_only(v):
    return v * (0.5 + 0.5 * jnp.tanh(ROOT * v * (1.0 + CUBE * v * v)))


def swapped(x, flips):
    rows = lax.broadcasted_iota(jnp.int32, x.shape, 0)
    for bit in (1, 2, 4):
        down, up = pltpu.roll(x, SEGS - bit, 0), pltpu.roll(x, bit, 0)
        turned = jnp.where((rows & bit) == 0, down, up)
        x = jnp.where((flips & bit) != 0, turned, x)
    return x


def exclusive(prod, last, flips, backward):
    prod, last = swapped(prod, flips), swapped(last, flips)
    one = jnp.ones((1, WIDE), jnp.float32)
    zero = jnp.zeros((1, WIDE), jnp.float32)
    coef, base = [one], [zero]
    order = range(SEGS - 1, -1, -1) if backward else range(SEGS)
    for s in order:
        coef.append(prod[s : s + 1] * coef[-1])
        base.append(prod[s : s + 1] * base[-1] + last[s : s + 1])
    total = jnp.concatenate([coef[-1], base[-1]] + [zero] * (SEGS - 2), axis=0)
    coef, base = coef[:-1], base[:-1]
    if backward:
        coef, base = coef[::-1], base[::-1]
    return (
        swapped(jnp.concatenate(coef, axis=0), flips),
        swapped(jnp.concatenate(base, axis=0), flips),
        total,
    )


def lay_out(blocks, whole):
    size = whole.shape[0] // len(blocks)
    for b, block in enumerate(blocks):
        whole[b * size : (b + 1) * size, :] = block[...]


def enter_kernel(
    parts, where, edge, code, small, gates, *rest
):
    inter, v_out, rg_out, ig_out, e_out, sq_out, maps, total, u = rest[parts:]
    lay_out(rest[:parts], u)
    rows = u.shape[0]
    steps = rows // SEGS
    flips = where[0]

    def lay(s, carry):
        inter[pl.ds(pl.multiple_of(24 + 8 * s, 8), 8), :] = u[pl.ds(s, 8, stride=steps), :]
        return carry

    lax.fori_loop(0, steps, lay, 0, unroll=8)
    first = lax.broadcasted_iota(jnp.int32, (SEGS, WIDE), 0) == 0
    for j in range(3):
        nat = pltpu.roll(swapped(inter[pl.ds(8 * (steps + j), 8), :], flips), 1, 0)
        nat = jnp.where(first, edge[5 + j : 6 + j, :], nat)
        inter[8 * j : 8 * j + 8, :] = swapped(nat, flips)

    def tile(i, carry):
        prod, state = carry
        base = pl.multiple_of(i * TILE, TILE)
        c = code[pl.ds(base, TILE), :]
        v = small[0:1, :] * inter[pl.ds(base + 24, TILE), :]
        for k in (1, 2, 3):
            v = v + jnp.where(
                c >= k, small[k : k + 1, :] * inter[pl.ds(base + 24 - 8 * k, TILE), :], 0.0
            )
        high = v.astype(jnp.bfloat16)
        low = (v - high.astype(jnp.float32)).astype(jnp.bfloat16)
        mat = gates[0]
        pre = jnp.dot(
            jnp.concatenate([high, low], axis=1),
            jnp.concatenate([mat, mat], axis=0),
            preferred_element_type=jnp.float32,
        )
        rg = 1.0 / (1.0 + jnp.exp(-(pre[:, :WIDE] + small[5:6, :])))
        ig = jax.nn.sigmoid(pre[:, WIDE:] + small[6:7, :])
        la = small[4:5, :] * rg
        e = jnp.exp(la)
        sq = jnp.sqrt(jnp.tanh(-la) * (1.0 + e * e))
        here = pl.ds(base, TILE)
        v_out[here, :] = v
        rg_out[here, :] = rg
        ig_out[here, :] = ig
        e_out[here, :] = e
        sq_out[here, :] = sq
        keep = jnp.where(c > 0, e, 0.0)
        inflow = sq * ig * v
        for s in range(TILE // SEGS):
            k = keep[8 * s : 8 * s + 8]
            prod = prod * k
            state = k * state + inflow[8 * s : 8 * s + 8]
        return prod, state

    prod, state = lax.fori_loop(
        0,
        rows // TILE,
        tile,
        (jnp.ones((SEGS, WIDE), jnp.float32), jnp.zeros((SEGS, WIDE), jnp.float32)),
    )
    coef, base, whole = exclusive(prod, state, flips, False)
    maps[0:8, :] = prod
    maps[8:16, :] = coef
    maps[16:24, :] = base
    total[...] = whole


def state_kernel(count, parts, where, v, ig, e, sq, code, maps, *rest):
    others, p_parts = rest[: count - 1], rest[count - 1 : count - 1 + parts]
    hs, out, wide, p = rest[count - 1 + parts :]
    lay_out(p_parts, p)
    rows = v.shape[0]
    steps = rows // SEGS
    mine = where[1]
    entry = jnp.zeros((1, WIDE), jnp.float32)
    for d in range(count - 1, 0, -1):
        piece = others[d - 1]
        entry = jnp.where(mine >= d, piece[0:1, :] * entry + piece[1:2, :], entry)
    state = maps[8:16, :] * entry + maps[16:24, :]
    hs[0:8, :] = state

    def tile(i, state):
        base = pl.multiple_of(i * TILE, TILE)
        here = pl.ds(base, TILE)
        keep = jnp.where(code[here, :] > 0, e[here, :], 0.0)
        inflow = sq[here, :] * ig[here, :] * v[here, :]
        for s in range(TILE // SEGS):
            state = keep[8 * s : 8 * s + 8] * state + inflow[8 * s : 8 * s + 8]
            hs[pl.ds(base + 8 * s + 8, 8), :] = state
            there = pl.ds(i * (TILE // SEGS) + s, 8, stride=steps)
            wide[there, :] = state * gelu_only(p[there, :])
        return state

    lax.fori_loop(0, rows // TILE, tile, state)
    out[...] = wide[...].astype(jnp.bfloat16)


def adjoint_kernel(parts, p_count, where, hs, e, code, maps, *rest):
    dhs, dp, back, total, wide, do, p = rest[parts + p_count :]
    lay_out(rest[:parts], do)
    lay_out(rest[parts : parts + p_count], p)
    rows = do.shape[0]
    steps = rows // SEGS
    flips = where[0]

    def tile(i, grad):
        i = rows // TILE - 1 - i
        base = pl.multiple_of(i * TILE, TILE)
        keep = jnp.where(code[pl.ds(base, TILE), :] > 0, e[pl.ds(base, TILE), :], 0.0)
        for s in range(TILE // SEGS - 1, -1, -1):
            there = pl.ds(i * (TILE // SEGS) + s, 8, stride=steps)
            d = do[there, :]
            act, slope = gelu_pair(p[there, :])
            wide[there, :] = d * hs[pl.ds(base + 8 * s + 8, 8), :] * slope
            dh = d * act
            dhs[pl.ds(base + 8 * s, 8), :] = dh
            grad = keep[8 * s : 8 * s + 8] * (dh + grad)
        return grad

    grad = lax.fori_loop(0, rows // TILE, tile, jnp.zeros((SEGS, WIDE), jnp.float32))
    dp[...] = wide[...].astype(jnp.bfloat16)
    coef, base, whole = exclusive(maps[0:8, :], grad, flips, True)
    back[0:8, :] = coef
    back[8:16, :] = base
    total[...] = whole


def leave_kernel(count, where, dhs, inter, v, rg, ig, e, sq, hs, code, small, gates_t, back, *rest):
    products, grads = rest[: count - 1], rest[count - 1 : 2 * count - 2]
    du, grad_gates, sums, edge, dv_all, wide = rest[2 * count - 1 :]
    rows = dhs.shape[0]
    steps = rows // SEGS
    flips, mine = where[0], where[1]
    entry = jnp.zeros((1, WIDE), jnp.float32)
    for j in range(count - 1, 0, -1):
        d = count - j
        entry = jnp.where(
            mine + j < count, products[d - 1][0:1, :] * entry + grads[d - 1][1:2, :], entry
        )
    grad = back[0:8, :] * entry + back[8:16, :]
    grad_gates[...] = jnp.zeros_like(grad_gates)

    def fold(x):
        parts = [x[8 * s : 8 * s + 8] for s in range(TILE // SEGS)]
        while len(parts) > 1:
            parts = [a + b for a, b in zip(parts[::2], parts[1::2])]
        return parts[0]

    def tile(i, carry):
        grad, taps, decay, shift_a, shift_i = carry
        i = rows // TILE - 1 - i
        base = pl.multiple_of(i * TILE, TILE)
        here = pl.ds(base, TILE)
        c = code[here, :]
        e_now, sq_now, rg_now, ig_now, v_now = e[here, :], sq[here, :], rg[here, :], ig[here, :], v[here, :]
        keep = jnp.where(c > 0, e_now, 0.0)
        d_now = dhs[here, :]
        pieces = [None] * (TILE // SEGS)
        for s in range(TILE // SEGS - 1, -1, -1):
            a = d_now[8 * s : 8 * s + 8] + grad
            pieces[s] = a
            grad = keep[8 * s : 8 * s + 8] * a
        a = jnp.concatenate(pieces, axis=0)
        q = ig_now * v_now
        dla = a * (keep * hs[here, :] - q * (e_now * e_now) / jnp.maximum(sq_now, 1e-25))
        rate = rg_now * dla
        decay = decay + fold(rate)
        dra = small[4:5, :] * rate * (1.0 - rg_now)
        asq = a * sq_now
        dia = asq * q * (1.0 - ig_now)
        shift_a = shift_a + fold(dra)
        shift_i = shift_i + fold(dia)
        both = jnp.concatenate([dra.astype(jnp.bfloat16), dia.astype(jnp.bfloat16)], axis=1)
        dv = asq * ig_now + jnp.dot(both, gates_t[0], preferred_element_type=jnp.float32)
        grad_gates[0] += lax.dot_general(
            v_now.astype(jnp.bfloat16),
            both,
            (((0,), (0,)), ((), ())),
            preferred_element_type=jnp.float32,
        )
        dv_all[here, :] = dv
        new_taps = [taps[0] + fold(dv * inter[pl.ds(base + 24, TILE), :])]
        for k in (1, 2, 3):
            new_taps.append(
                taps[k]
                + fold(jnp.where(c >= k, dv * inter[pl.ds(base + 24 - 8 * k, TILE), :], 0.0))
            )
        return grad, tuple(new_taps), decay, shift_a, shift_i

    zero = jnp.zeros((SEGS, WIDE), jnp.float32)
    _, taps, decay, shift_a, shift_i = lax.fori_loop(
        0, rows // TILE, tile, (grad, (zero,) * 4, zero, zero, zero)
    )
    totals = [jnp.sum(x, axis=0, keepdims=True) for x in (*taps, decay, shift_a, shift_i)]
    sums[...] = jnp.concatenate(totals + [jnp.zeros((1, WIDE), jnp.float32)], axis=0)
    last = lax.broadcasted_iota(jnp.int32, (SEGS, WIDE), 0) == SEGS - 1
    edges = []
    for j in range(3):
        nat = swapped(dv_all[8 * j : 8 * j + 8, :], flips)
        edges.append(nat[0:1])
        nat = jnp.where(last, 0.0, pltpu.roll(nat, SEGS - 1, 0))
        dv_all[pl.ds(rows + 8 * j, 8), :] = swapped(nat, flips)
    edge[...] = jnp.concatenate(edges + [jnp.zeros((SEGS - 3, WIDE), jnp.float32)], axis=0)

    def mix(i, carry):
        base = pl.multiple_of(i * TILE, TILE)
        total = small[0:1, :] * dv_all[pl.ds(base, TILE), :]
        for k in (1, 2, 3):
            there = pl.ds(base + 8 * k, TILE)
            total = total + jnp.where(
                code[there, :] >= k, small[k : k + 1, :] * dv_all[there, :], 0.0
            )
        for s in range(TILE // SEGS):
            wide[pl.ds(i * (TILE // SEGS) + s, 8, stride=steps), :] = total[8 * s : 8 * s + 8]
        return carry

    lax.fori_loop(0, rows // TILE, mix, 0)
    du[...] = wide[...].astype(jnp.bfloat16)


def copy_kernel(pick, x, out):
    out[...] = x[0, 0]


def reordered(pick, x, name):
    _, segs, rows, width = x.shape
    return pl.pallas_call(
        copy_kernel,
        grid_spec=pltpu.PrefetchScalarGridSpec(
            num_scalar_prefetch=1,
            grid=(segs,),
            in_specs=[pl.BlockSpec((1, 1, rows, width), lambda s, p: (p[1], s ^ p[0], 0, 0))],
            out_specs=pl.BlockSpec((rows, width), lambda s, p: (s, 0)),
        ),
        out_shape=jax.ShapeDtypeStruct((segs * rows, width), x.dtype),
        cost_estimate=cost(0.3),
        name=name,
    )(pick, x)


def nt(left_mat, right_mat):
    return lax.dot_general(
        left_mat, right_mat, (((1,), (1,)), ((), ())), preferred_element_type=jnp.float32
    )


def cost(us):
    return pl.CostEstimate(flops=int(us * 1e9), bytes_accessed=1, transcendentals=0)


def nt(left_mat, right_mat):
    return lax.dot_general(
        left_mat, right_mat, (((1,), (1,)), ((), ())), preferred_element_type=jnp.float32
    )


def mlp_kernel(h, dy, wg, wu, wd, mid, low_gate, low_up, part):
    up_pre = nt(h[...], wu[...])
    act, slope = gelu_pair(nt(h[...], wg[...]))
    grad_mid = nt(dy[...], wd[...])
    mid[...] = (act * up_pre).astype(jnp.bfloat16)
    low_gate[...] = (grad_mid * (up_pre * slope)).astype(jnp.bfloat16)
    low_up[...] = (grad_mid * act).astype(jnp.bfloat16)
    part[...] = (
        jnp.dot(low_gate[...], wg[...], preferred_element_type=jnp.float32)
        + jnp.dot(low_up[...], wu[...], preferred_element_type=jnp.float32)
    ).astype(part.dtype)


def mlp(h, cot, block, wg, wu, wd, kind):
    rows, width = h.shape
    hidden = wg.shape[0]
    step = min(rows, 256)
    count = rows // step
    row_spec = pl.BlockSpec((step, width), lambda j: (j, 0))
    cot_spec = pl.BlockSpec((step, width), lambda j: (j + block * count, 0))
    weight = pl.BlockSpec((hidden, width), lambda j: (0, 0))
    act = pl.BlockSpec((step, hidden), lambda j: (j, 0))
    low_shape = jax.ShapeDtypeStruct((rows, hidden), jnp.bfloat16)
    wg, wu, wd = (pltpu.with_memory_space_constraint(w, pltpu.VMEM) for w in (wg, wu, wd))
    return pl.pallas_call(
        mlp_kernel,
        grid=(count,),
        in_specs=[row_spec, cot_spec, weight, weight, weight],
        out_specs=[act, act, act, row_spec],
        out_shape=[low_shape] * 3 + [jax.ShapeDtypeStruct((rows, width), kind)],
        compiler_params=pltpu.CompilerParams(vmem_limit_bytes=24 * 2**20),
        cost_estimate=cost(0.3),
        name="mlp",
    )(h, cot, wg, wu, wd)


CHUNK = 192


def grads_kernel(spans, lefts, which, cuts, added, *refs):
    rights = [refs[lefts + i] for i in which]
    more = refs[lefts + max(which) + 1 :][:added]
    outs = refs[lefts + max(which) + 1 + added :]
    count, _, part = outs[0].shape
    at = 0
    for left, right, (low_col, high_col) in zip(refs[:lefts], rights, spans):
        first = low_col // WIDE * WIDE
        last = min(-(-high_col // WIDE) * WIDE, left.shape[1])
        total = lax.dot_general(
            left[:, first:last],
            right[...],
            (((0,), (0,)), ((), ())),
            preferred_element_type=jnp.float32,
        )
        done = 0
        while done < high_col - low_col:
            size = min(cuts, high_col - low_col - done)
            rows = low_col - first + done
            for z in range(count):
                piece = total[rows : rows + size, z * part : (z + 1) * part]
                if added:
                    piece = piece + more[at // cuts][z].astype(jnp.float32)
                if len(outs) > 1:
                    outs[at // cuts][z] = piece.astype(jnp.bfloat16)
                else:
                    outs[0][z, at : at + size, :] = piece.astype(jnp.bfloat16)
            done += size
            at += size


def grads(pairs, half, halves, count, split=False, added=()):
    spans, rows = [], 0
    for left, _ in pairs:
        size = left.shape[1] // halves
        spans.append((half * size, (half + 1) * size))
        rows += size
    part = pairs[0][1].shape[1] // count
    sizes = [b - a for a, b in spans]
    cuts = rows if len(sizes) == 1 else 16
    if split or added:
        cuts = next(c for c in (CHUNK, 128, 64, 16) if all(s % c == 0 for s in sizes))
    rights, which = [], []
    for _, right in pairs:
        if not any(right is r for r in rights):
            rights.append(right)
        which.append(next(i for i, r in enumerate(rights) if r is right))
    args = [p[0] for p in pairs] + rights + list(added)
    shape = (count, cuts if split else rows, part)
    return pl.pallas_call(
        functools.partial(grads_kernel, spans, len(pairs), which, cuts, len(added)),
        out_shape=[jax.ShapeDtypeStruct(shape, jnp.bfloat16)] * (rows // cuts if split else 1),
        compiler_params=pltpu.CompilerParams(vmem_limit_bytes=32 * 2**20),
        cost_estimate=cost(0.3),
        name="grads",
    )(*args)


def lanes(rows, offset=0):
    return pl.BlockSpec((rows, WIDE), lambda n: (0, n + offset))


def paths(rows, groups, halves, offset):
    size = groups // halves
    return pl.BlockSpec((rows, WIDE), lambda n: (0, n + (n // size + offset) * size))


def per_block(shape):
    return pl.BlockSpec((1,) + shape, lambda n: (n, 0, 0))


def scalars():
    return pl.BlockSpec(memory_space=pltpu.SMEM)


def shared(shape):
    return pl.BlockSpec(shape, lambda n: (0,) * len(shape))


def launch(kernel, groups, in_specs, outs, scratch, args, name, aliases={}):
    def place(shape, dtype):
        if shape[0] >= 512 and (dtype == jnp.float32 or shape[1] == 2 * groups * WIDE):
            return pltpu.HBM(shape, dtype)
        return jax.ShapeDtypeStruct(shape, dtype)

    def pin(a):
        if a.shape[0] >= 512 and a.shape[1] > WIDE and (
            a.dtype == jnp.float32 or a.shape[1] == 2 * groups * WIDE
        ):
            return pltpu.with_memory_space_constraint(a, pltpu.HBM)
        return a

    return pl.pallas_call(
        kernel,
        grid=(groups,),
        in_specs=in_specs,
        out_specs=[spec for _, _, spec in outs],
        out_shape=[place(shape, dtype) for shape, dtype, _ in outs],
        scratch_shapes=scratch,
        compiler_params=pltpu.CompilerParams(vmem_limit_bytes=16 * 2**20),
        cost_estimate=cost(0.3),
        name=name,
        input_output_aliases=aliases,
    )(*[pin(a) for a in args])


def enter(where, both, edge, code, small, gates, halves):
    parts, size = len(both), both[0].shape[0]
    rows, channels = parts * size, both[0].shape[1] // 2
    groups = channels // WIDE
    f32 = jnp.float32
    full = ((rows, channels), f32, lanes(rows))
    return launch(
        functools.partial(enter_kernel, parts),
        groups,
        [
            scalars(),
            paths(8, groups, halves, 0),
            shared(code.shape),
            lanes(8),
            per_block((WIDE, 2 * WIDE)),
        ]
        + [paths(size, groups, halves, 0)] * parts,
        [
            ((rows + 24, channels), f32, lanes(rows + 24)),
            full,
            full,
            full,
            full,
            full,
            ((24, channels), f32, lanes(24)),
            ((8, channels), f32, lanes(8)),
        ],
        [pltpu.VMEM((rows, WIDE), f32)],
        (where, edge, code, small, gates, *both),
        "enter",
    )


def states_of(where, v, ig, e, sq, code, both, maps, others, halves):
    rows, channels = v.shape
    parts, size = len(both), both[0].shape[0]
    groups = channels // WIDE
    f32 = jnp.float32
    return launch(
        functools.partial(state_kernel, len(others) + 1, parts),
        groups,
        [scalars()]
        + [lanes(rows)] * 4
        + [shared(code.shape), lanes(24)]
        + [lanes(8)] * len(others)
        + [paths(size, groups, halves, 1)] * parts,
        [
            ((rows + 8, channels), f32, lanes(rows + 8)),
            ((rows, channels), jnp.bfloat16, lanes(rows)),
        ],
        [pltpu.VMEM((rows, WIDE), f32)] * 2,
        (where, v, ig, e, sq, code, maps, *others, *both),
        "states",
    )


def adjoints(where, do, both, hs, e, code, maps, halves):
    parts, (size, channels) = len(do), do[0].shape
    p_count, p_size = len(both), both[0].shape[0]
    rows = parts * size
    groups = channels // WIDE
    f32 = jnp.float32
    return launch(
        functools.partial(adjoint_kernel, parts, p_count),
        groups,
        [scalars(), lanes(rows + 8), lanes(rows), shared(code.shape), lanes(24)]
        + [lanes(size)] * parts
        + [paths(p_size, groups, halves, 1)] * p_count,
        [
            ((rows, channels), f32, lanes(rows)),
            ((rows, 2 * channels), jnp.bfloat16, paths(rows, groups, halves, 1)),
            ((16, channels), f32, lanes(16)),
            ((8, channels), f32, lanes(8)),
        ],
        [pltpu.VMEM((rows, WIDE), f32)] * 3,
        (where, hs, e, code, maps, *do, *both),
        "adjoint",
    )


def leave(where, dhs, kept, hs, code, small, gates_t, back, products, grads, half_done, halves):
    inter, v, rg, ig, e, sq = kept
    rows, channels = dhs.shape
    groups = channels // WIDE
    f32 = jnp.float32
    count = len(products) + 1
    return launch(
        functools.partial(leave_kernel, count),
        groups,
        [scalars(), lanes(rows), lanes(rows + 24)]
        + [lanes(rows)] * 5
        + [
            lanes(rows + 8),
            shared(code.shape),
            lanes(8),
            per_block((2 * WIDE, WIDE)),
            lanes(16),
        ]
        + [lanes(8)] * (2 * count - 2)
        + [pl.BlockSpec(memory_space=pl.ANY)],
        [
            ((rows, 2 * channels), jnp.bfloat16, paths(rows, groups, halves, 0)),
            ((groups, WIDE, 2 * WIDE), f32, per_block((WIDE, 2 * WIDE))),
            ((8, channels), f32, lanes(8)),
            ((8, channels), f32, lanes(8)),
        ],
        [pltpu.VMEM((rows + 24, WIDE), f32), pltpu.VMEM((rows, WIDE), f32)],
        (where, dhs, inter, v, rg, ig, e, sq, hs, code, small, gates_t, back, *products, *grads, half_done),
        "leave",
        {11 + 2 * count: 0},
    )


def dense(left_mat, right_mat):
    return jnp.dot(left_mat, right_mat, preferred_element_type=jnp.float32)


def dense_nt(left_mat, right_mat):
    return lax.dot_general(
        left_mat, right_mat, (((1,), (1,)), ((), ())), preferred_element_type=jnp.float32
    )


def dense_tn(left_mat, right_mat):
    return lax.dot_general(
        left_mat, right_mat, (((0,), (0,)), ((), ())), preferred_element_type=jnp.float32
    )


def low(x):
    return x.astype(jnp.bfloat16)


def high(x):
    return x.astype(jnp.float32)


def after(x, *others):
    return lax.optimization_barrier((x,) + others)[0]


def tied(*values):
    return lax.optimization_barrier(values)


def turned(x, axis, distance):
    count = lax.axis_size(axis)
    return lax.ppermute(x, axis, [(i, (i + distance) % count) for i in range(count)])


def around(x, axis):
    return [turned(x, axis, d) for d in range(1, lax.axis_size(axis))]


def in_order(x, pieces, axis):
    count = lax.axis_size(axis)
    mine = lax.axis_index(axis)
    turn = jnp.stack([x] + pieces[::-1])
    turn = jnp.concatenate([turn, turn], axis=0)
    return lax.dynamic_slice_in_dim(turn, (count - mine) % count, count, 0)


def flip(x, bits):
    count = lax.axis_size("mp")
    return lax.ppermute(x, "mp", [(i, i ^ bits) for i in range(count)])


class Paired:
    halves = 2
    blocks = 4

    def spread(self, rows):
        half = rows.shape[0] // 2
        a, b = rows[:half], rows[half:]
        xb, ya = flip(b, 2), flip(a, 4)
        xa, yb = flip(a, 2), flip(b, 4)
        da, db = flip(ya, 2), flip(xb, 4)
        pairs = ((xa, xb), (ya, yb), (da, db))
        return [rows] + [jnp.concatenate(p, axis=0) for p in pairs], (da, db)

    def give(self, part, block):
        return part if block == 0 else flip(part, 2 * block)

    def gather_sum(self, pieces):
        total = high(pieces[0])
        for piece in pieces[1:]:
            total = total + high(piece)
        return total

    def collect(self, part):
        p3 = low(part(3))
        half = p3.shape[0] // 2
        r2a, r1b = flip(p3[:half], 2), flip(p3[half:], 4)
        p1, p2 = part(1), part(2)
        s1a, s2b = flip(low(p1[:half]), 2), flip(low(p2[half:]), 4)
        p0 = part(0)
        s2a = flip(low(high(p2[:half]) + high(r2a)), 4)
        s1b = flip(low(high(p1[half:]) + high(r1b)), 2)
        return (p0, s1a, s1b, s2a, s2b), (r2a, r1b)

    def finish(self, pieces):
        p0, s1a, s1b, s2a, s2b = pieces
        far = [
            jnp.concatenate([s1a, s1b], axis=0),
            jnp.concatenate([s2a, s2b], axis=0),
        ]
        return high(p0) + high(far[0]) + high(far[1])

    def both(self, x):
        return [x, flip(x, 1)]

    def sent_totals(self, pairs, count):
        return [flip(x, 1) for x in grads(pairs, 1, 2, count, split=True)]

    def own_totals(self, pairs, count, sent):
        return grads(pairs, 0, 2, count, added=sent)[0]

    def owner_small(self, grad_gates, lines, gains):
        blocks, channels = grad_gates.shape[0] // 2, lines.shape[1] // 2
        grad_gates = grad_gates[:blocks] + flip(grad_gates[blocks:], 1)
        lines = lines[:, :channels] + flip(lines[:, channels:], 1)
        return small_sums(grad_gates, lines, gains)

    def plane_sum(self, gains):
        for bits in (1, 2, 4):
            gains = gains + flip(gains, bits)
        return gains


class Plain:
    halves = 1
    blocks = 1

    def spread(self, rows):
        rows = lax.all_gather(rows, "mp", axis=0, tiled=True)
        return [rows], (rows,)

    def collect(self, part):
        rows = lax.psum_scatter(low(part(0)), "mp", scatter_dimension=0, tiled=True)
        return (rows,), (rows,)

    def finish(self, pieces):
        return high(pieces[0])

    def both(self, x):
        return [x]

    def sent_totals(self, pairs, count):
        return []

    def own_totals(self, pairs, count, sent):
        return grads(pairs, 0, 1, count)[0]

    def owner_small(self, grad_gates, lines, gains):
        return small_sums(grad_gates, lines, gains)

    def plane_sum(self, gains):
        return lax.psum(gains, "mp")


def small_sums(grad_gates, lines, gains):
    count, seq_rank = lax.axis_size("seq"), lax.axis_index("seq")
    blocks = grad_gates.shape[0]
    depth, thin, part = WIDE // count, lines.shape[1] // count, gains.shape[1] // count
    pieces = jnp.concatenate(
        [
            grad_gates.reshape(blocks, count, depth, 2 * WIDE).transpose(1, 0, 2, 3).reshape(count, -1),
            lines.reshape(-1, count, thin).transpose(1, 0, 2).reshape(count, -1),
            gains.reshape(2, count, part).transpose(1, 0, 2).reshape(count, -1),
        ],
        axis=1,
    )
    size = pieces.shape[1]
    pieces = jnp.pad(pieces, ((0, 0), (0, -size % 1024))).reshape(count, -1, WIDE)
    total = lax.dynamic_index_in_dim(pieces, seq_rank, 0, keepdims=False)
    for d in range(1, count):
        piece = lax.dynamic_index_in_dim(pieces, (seq_rank + d) % count, 0, keepdims=False)
        total = total + turned(piece, "seq", d)
    total = total.reshape(-1)
    at = blocks * depth * 2 * WIDE
    sum_gates = total[:at].reshape(blocks, depth, 2, WIDE)
    lines = total[at : at + 7 * thin].reshape(7, thin)
    at += 7 * thin
    return sum_gates, lines, total[at : at + 2 * part].reshape(2, part)


def mask_code(starts_row, first_pos, flips, steps):
    shape = ((steps + 3) * SEGS, WIDE)
    row = lax.broadcasted_iota(jnp.int32, shape, 0)
    places = first_pos + ((row & (SEGS - 1)) ^ flips) * steps + (row // SEGS)
    code = jnp.full(shape, 4, jnp.int32)
    for e in range(starts_row.shape[0]):
        away = places - starts_row[e]
        code = jnp.where((starts_row[e] > 0) & (away >= 0), jnp.minimum(code, away), code)
    return code.astype(jnp.float32)


def normed(rows):
    scale = lax.rsqrt(jnp.mean(rows * rows, axis=-1, keepdims=True) + epsilon)
    return rows * scale, scale


def norm_back(grad_norm, norm, scale):
    return scale * (grad_norm - norm * jnp.mean(grad_norm * norm, axis=-1, keepdims=True))


def small_weights(gate_a, gate_i, conv_w, decay_param, bias_a, bias_i, gain_one, gain_two):
    blocks, depth, _ = gate_a.shape
    taps, thin = conv_w.shape
    part = gain_one.shape[0]
    count = lax.axis_size("seq")
    if part % WIDE == 0 and thin <= WIDE:
        lines = jnp.concatenate([conv_w, decay_param[None], bias_a[None], bias_i[None]], axis=0)
        lines = jnp.pad(lines, ((0, 1), (0, WIDE - thin)))
        gains = jnp.concatenate([gain_one.reshape(-1, WIDE), gain_two.reshape(-1, WIDE)], axis=0)
        pack = jnp.concatenate(
            [gate_a.reshape(-1, WIDE), gate_i.reshape(-1, WIDE), lines, gains], axis=0
        )
        pack = jnp.pad(pack, ((0, -pack.shape[0] % 16), (0, 0)))
        pack = in_order(pack, around(pack, "seq"), "seq")
        at = blocks * depth
        ga, gi = (
            pack[:, i * at : (i + 1) * at].reshape(count, blocks, depth, WIDE).transpose(1, 0, 2, 3)
            for i in (0, 1)
        )
        ga, gi = (x.reshape(blocks, count * depth, WIDE) for x in (ga, gi))
        lines = pack[:, 2 * at : 2 * at + taps + 3, :thin].transpose(1, 0, 2).reshape(taps + 3, -1)
        at = 2 * at + taps + 4
        size = part // WIDE
        gain_one = pack[:, at : at + size].reshape(-1)
        gain_two = pack[:, at + size : at + 2 * size].reshape(-1)
    else:
        ga, gi = (lax.all_gather(x, "seq", axis=1, tiled=True) for x in (gate_a, gate_i))
        lines = jnp.concatenate([conv_w, decay_param[None], bias_a[None], bias_i[None]], axis=0)
        lines = lax.all_gather(lines, "seq", axis=1, tiled=True)
        gain_one, gain_two = (
            lax.all_gather(x, "seq", axis=0, tiled=True) for x in (gain_one, gain_two)
        )
    return jnp.concatenate([ga, gi], axis=2), high(lines), high(gain_one), high(gain_two)


def micro(plan, where, flips, stream, cot, starts_row, weights):
    first, pack, smalls = weights
    count = stream.shape[0] * lax.axis_size("mp") // plan.halves
    steps = count // SEGS
    size = count // plan.blocks
    blocks_of_z = lax.axis_size("seq")
    seq_rank = lax.axis_index("seq")
    wide = plan.halves
    def rows_of(x, b):
        return x[b * size : (b + 1) * size]

    n1, s1 = normed(stream)
    low_n1 = low(n1)
    h1, _ = plan.spread(low_n1)
    second = lax.all_gather(pack, "seq", axis=1, tiled=True)
    come = h1[min(1, plan.blocks - 1)]
    starts_row = after(starts_row, come)
    code = mask_code(starts_row, seq_rank * count, flips, steps)
    gates, lines, gain_one, gain_two = small_weights(*after(smalls, come))
    gates = jnp.concatenate(plan.both(gates), axis=0)
    lines = jnp.concatenate(plan.both(lines), axis=1)
    taps, decay = lines[:4], lines[4]
    channels = lines.shape[1]
    own = channels // wide
    rate = -8.0 * jax.nn.softplus(decay)
    small = jnp.concatenate([taps, rate[None], lines[5:7], jnp.zeros((1, channels))], axis=0)
    gates_t = jnp.concatenate(
        [gates[:, :, :WIDE].transpose(0, 2, 1), gates[:, :, WIDE:].transpose(0, 2, 1)], axis=1
    )
    h1 = jnp.concatenate([low(high(h) * gain_one) for h in h1], axis=0)
    other = plan.both(after(first, h1, code, small, gates, gates_t, pack))
    wxy = jnp.concatenate([x[i] for x in other for i in (0, 1)], axis=0)
    wo = jnp.concatenate([x[2] for x in other], axis=0)
    up_both = [dense_nt(rows_of(h1, b), wxy) for b in range(plan.blocks)]
    last = lax.dynamic_slice_in_dim(h1, ((SEGS - 1) ^ flips) * steps + steps - 8, 8, 0)
    before = turned(last, "seq", 1)
    edge = jnp.where(seq_rank > 0, dense_nt(before, wxy), 0.0)
    *kept, maps, total = enter(where, up_both, edge, code, small, gates, wide)
    inter, v, rg, ig, e, sq = kept
    fore = around(total, "seq")
    hs, mixed = states_of(where, v, ig, e, sq, code, up_both, maps, fore, wide)

    more, come = plan.collect(lambda b: dense(rows_of(mixed, b), wo))
    cot = cot(come[0])
    middle = stream + plan.finish(after(more, cot))
    n2, s2 = normed(middle)
    h2, come = plan.spread(low(n2 * gain_two))
    second = after(second, *come)
    third = second.shape[0] // 3
    wg, wu, wd = (
        jnp.concatenate(plan.both(second[i * third : (i + 1) * third]), axis=0) for i in range(3)
    )
    each = range(plan.blocks)
    found = {}
    for b in list(each)[::-1]:
        kind = jnp.float32 if b == 0 and plan.blocks > 1 else jnp.bfloat16
        found[b] = mlp(h2[b], cot, b, wg, wu, wd, kind)
    back_two, come = plan.collect(lambda b: found[b][3])
    mid, low_gate, low_up = (
        jnp.concatenate([found[b][i] for b in each], axis=0) for i in (0, 1, 2)
    )
    h2 = jnp.concatenate(h2, axis=0)
    mid = after(mid, *come)
    low_gate = after(low_gate, *back_two[1:])
    sent_wd = plan.sent_totals([(mid, cot)], blocks_of_z)
    pack_wd = plan.own_totals([(mid, cot)], blocks_of_z, sent_wd)
    grad_wd = owner_sum(pack_wd)
    pairs = [(low_gate, h2), (low_up, h2)]
    sent_gate_up = plan.sent_totals(pairs, blocks_of_z)
    back_two = plan.finish(after(back_two, pack_wd, *sent_gate_up))
    grad_two = jnp.sum(back_two * n2, axis=0)
    grad_middle = high(cot_rows_of(plan, cot, stream.shape[0])) + norm_back(
        back_two * gain_two, n2, s2
    )
    low_middle = low(grad_middle)
    mid_rows, _ = plan.spread(low_middle)
    pairs = [(after(low_gate, low_middle), h2), (low_up, h2)]
    pack_gate_up = plan.own_totals(pairs, blocks_of_z, sent_gate_up)
    grad_gate_up = owner_sum(pack_gate_up)
    shares = dense(after(mid, pack_gate_up), wd)
    shares = [rows_of(shares, b) for b in each]
    shares = [x if b == 0 else low(x) for b, x in enumerate(shares)]
    mid_rows = after(jnp.concatenate(mid_rows, axis=0), *shares)
    do = [dense_nt(mid_rows, wo)]
    block_parts, _ = plan.collect(lambda b: after(shares[b], do[0]))
    dhs, dup, back, total = adjoints(where, do, up_both, hs, e, code, maps, wide)
    aft = around(total, "seq")
    dhs, grad_wd = tied(dhs, grad_wd)
    dup, grad_gates, sums, edge = leave(
        where, dhs, kept, hs, code, small, gates_t, back, fore, aft, dup, wide
    )
    nxt = jnp.where(seq_rank < lax.axis_size("seq") - 1, turned(edge, "seq", -1), 0.0)
    spots = [(steps + j) * SEGS + ((SEGS - 1) ^ flips) for j in range(3)]
    far = jnp.concatenate([lax.dynamic_slice(code, (i, 0), (1, 1)) for i in spots], axis=0)
    extra = [jnp.zeros((5, channels))]
    for j in range(3):
        row = jnp.zeros((1, channels))
        for k in range(3 - j, 4):
            i = j + k - 3
            row = row + jnp.where(far[i : i + 1] >= k, taps[k : k + 1] * nxt[i : i + 1], 0.0)
        extra.append(row)
    extra = jnp.concatenate(extra, axis=0)
    at = ((SEGS - 1) ^ flips) * steps + steps - 8
    extra = low(interleaved(extra, jnp.zeros_like(extra), wide))
    patch = low(high(lax.dynamic_slice_in_dim(dup, at, 8, 0)) + high(extra))
    dup = lax.dynamic_update_slice_in_dim(dup, patch, at, 0)
    pairs = [(dup, h1), (mixed, mid_rows)]
    pack_late = plan.own_totals(pairs, blocks_of_z, plan.sent_totals(pairs, blocks_of_z))
    dup, pack_late = tied(dup, pack_late)
    parts = {b: dense(rows_of(dup, b), wxy) for b in list(each)[::-1]}
    back_one, _ = plan.collect(lambda b: parts[b])
    grad_one = sum(jnp.sum(parts[b] * high(rows_of(h1, b)), axis=0) for b in parts) / gain_one
    pack_late, grad_gate_up = tied(pack_late, grad_gate_up)
    late = owner_sum(pack_late)
    decay_sum = -8.0 * jax.nn.sigmoid(decay) * sums[4]
    lines = jnp.concatenate([sums[:4], decay_sum[None], sums[5:7]], axis=0)
    little = plan.owner_small(grad_gates, lines, jnp.stack([grad_one, grad_two]))
    back_one = plan.finish(back_one)
    grad_rows = low(grad_middle + norm_back(back_one * gain_one, n1, s1))
    block_rows = low(middle + plan.finish(after(block_parts, little[2])))
    little = little[:2] + (plan.plane_sum(after(little[2], grad_rows)),)
    large = tuple(high(x) for x in (late, grad_gate_up, grad_wd))
    return block_rows, grad_rows, large, little


def interleaved(first, second, halves):
    size = first.shape[1] // halves
    return jnp.concatenate(
        [x[:, i * size : (i + 1) * size] for i in range(halves) for x in (first, second)], axis=1
    )


def cot_rows_of(plan, cot, rows):
    if plan.halves == 2:
        return cot[:rows]
    return lax.dynamic_slice_in_dim(cot, lax.axis_index("mp") * rows, rows, 0)


def owner_sum(pack):
    return lax.psum_scatter(pack, "seq", scatter_dimension=0, tiled=False)


def on_device(
    tokens,
    cotangent,
    w_x,
    w_y,
    w_out,
    w_gate,
    w_up,
    w_down,
    gate_a,
    gate_i,
    conv_w,
    decay_param,
    bias_a,
    bias_i,
    gain_one,
    gain_two,
    doc_starts,
):
    micros, own_rows, _ = tokens.shape
    span = cotangent.shape[1]
    count = lax.axis_size("seq")
    seq_rank = lax.axis_index("seq")
    mp_rank = lax.axis_index("mp")
    paired = micros == 2 and lax.axis_size("mp") == SEGS and span == SEGS * own_rows
    plan = Paired() if paired else Plain()
    channels, hidden = w_x.shape[1], w_gate.shape[1]
    blocks, depth, _ = gate_a.shape
    part = w_x.shape[0]
    thin = conv_w.shape[1]

    first = lax.all_gather(
        jnp.stack([w_x.T, w_y.T, w_out]), "seq", axis=2, tiled=True
    )
    second = lax.optimization_barrier(jnp.concatenate([w_gate.T, w_up.T, w_down], axis=0))
    smalls = (gate_a, gate_i, conv_w, decay_param, bias_a, bias_i, gain_one, gain_two)
    weights = (first, second, smalls)

    if paired:
        core = mp_rank % 2
        mine = lax.dynamic_index_in_dim(tokens, core, 0, keepdims=False)
        other = flip(lax.dynamic_index_in_dim(tokens, 1 - core, 0, keepdims=False), 1)
        stream = high(jnp.concatenate([mine, other], axis=0))
        pick = jnp.stack([mp_rank, core]).astype(jnp.int32)
        folded = cotangent.reshape(micros, SEGS, own_rows, -1)
        where = jnp.stack([mp_rank, seq_rank]).astype(jnp.int32)
        starts_row = lax.dynamic_index_in_dim(doc_starts, core, 0, keepdims=False)
        block_rows, grad_rows, large, little = micro(
            plan,
            where,
            mp_rank,
            stream,
            lambda come: reordered(after(pick, come), folded, "order"),
            starts_row,
            weights,
        )

        def returned(x):
            mine, other = x[:own_rows], flip(x[own_rows:], 1)
            return jnp.where(core == 0, jnp.stack([mine, other]), jnp.stack([other, mine]))

        block_all, grad_all = returned(block_rows), returned(grad_rows)
    else:
        where = jnp.stack([0 * seq_rank, seq_rank]).astype(jnp.int32)
        found = [
            micro(plan, where, 0, high(tokens[m]), lambda come, m=m: cotangent[m], doc_starts[m], weights)
            for m in range(micros)
        ]
        block_all = jnp.stack([f[0] for f in found])
        grad_all = jnp.stack([f[1] for f in found])
        large, little = jax.tree.map(lambda *x: sum(x), *[f[2:] for f in found])

    late, gate_up_grad, down_grad = large
    sum_gates, lines, gains = little
    return (
        block_all,
        grad_all,
        late[:channels].T,
        late[channels : 2 * channels].T,
        late[2 * channels :],
        gate_up_grad[:hidden].T,
        gate_up_grad[hidden:].T,
        down_grad,
        sum_gates[:, :, 0],
        sum_gates[:, :, 1],
        lines[:4],
        lines[4],
        lines[5],
        lines[6],
        gains[0],
        gains[1],
    )


def solution(mesh):
    return jax.shard_map(
        on_device,
        mesh=mesh,
        in_specs=(
            P(None, ("seq", "mp"), None),
            P(None, "seq", None),
            P("seq", "mp"),
            P("seq", "mp"),
            P("mp", "seq"),
            P("seq", "mp"),
            P("seq", "mp"),
            P("mp", "seq"),
            P("mp", "seq", None),
            P("mp", "seq", None),
            P(None, ("mp", "seq")),
            P(("mp", "seq")),
            P(("mp", "seq")),
            P(("mp", "seq")),
            P("seq"),
            P("seq"),
            P(),
        ),
        out_specs=(
            P(None, ("seq", "mp"), None),
            P(None, ("seq", "mp"), None),
            P("seq", "mp"),
            P("seq", "mp"),
            P("mp", "seq"),
            P("seq", "mp"),
            P("seq", "mp"),
            P("mp", "seq"),
            P("mp", "seq", None),
            P("mp", "seq", None),
            P(None, ("mp", "seq")),
            P(("mp", "seq")),
            P(("mp", "seq")),
            P(("mp", "seq")),
            P("seq"),
            P("seq"),
        ),
        check_vma=False,
    )
```

```python
import functools

import jax
import jax.numpy as jnp
from jax import lax
from jax.experimental import pallas as pl
from jax.experimental.pallas import tpu as pltpu
from jax.sharding import PartitionSpec as P

epsilon = 1e-06
SEGS = 8
WIDE = 128
TILE = 128
ROOT = 0.7978845608028654
CUBE = 0.044715


def gelu_pair(v):
    sq = v * v
    t = jnp.tanh(v * (ROOT + (ROOT * CUBE) * sq))
    half = 0.5 + 0.5 * t
    slope = half + (0.5 * v) * (1.0 - t * t) * (ROOT + (3.0 * CUBE * ROOT) * sq)
    return v * half, slope


def gelu_only(v):
    return v * (0.5 + 0.5 * jnp.tanh(ROOT * v * (1.0 + CUBE * v * v)))


def swapped(x, flips):
    rows = lax.broadcasted_iota(jnp.int32, x.shape, 0)
    for bit in (1, 2, 4):
        down, up = pltpu.roll(x, SEGS - bit, 0), pltpu.roll(x, bit, 0)
        turned = jnp.where((rows & bit) == 0, down, up)
        x = jnp.where((flips & bit) != 0, turned, x)
    return x


def exclusive(prod, last, flips, backward):
    prod, last = swapped(prod, flips), swapped(last, flips)
    one = jnp.ones((1, WIDE), jnp.float32)
    zero = jnp.zeros((1, WIDE), jnp.float32)
    coef, base = [one], [zero]
    order = range(SEGS - 1, -1, -1) if backward else range(SEGS)
    for s in order:
        coef.append(prod[s : s + 1] * coef[-1])
        base.append(prod[s : s + 1] * base[-1] + last[s : s + 1])
    total = jnp.concatenate([coef[-1], base[-1]] + [zero] * (SEGS - 2), axis=0)
    coef, base = coef[:-1], base[:-1]
    if backward:
        coef, base = coef[::-1], base[::-1]
    return (
        swapped(jnp.concatenate(coef, axis=0), flips),
        swapped(jnp.concatenate(base, axis=0), flips),
        total,
    )


def lay_out(blocks, whole):
    size = whole.shape[0] // len(blocks)
    for b, block in enumerate(blocks):
        whole[b * size : (b + 1) * size, :] = block[...]


def enter_kernel(
    parts, where, edge, code, small, gates, *rest
):
    inter, v_out, rg_out, ig_out, e_out, sq_out, maps, total, u = rest[parts:]
    lay_out(rest[:parts], u)
    rows = u.shape[0]
    steps = rows // SEGS
    flips = where[0]

    def lay(s, carry):
        inter[pl.ds(pl.multiple_of(24 + 8 * s, 8), 8), :] = u[pl.ds(s, 8, stride=steps), :]
        return carry

    lax.fori_loop(0, steps, lay, 0, unroll=8)
    first = lax.broadcasted_iota(jnp.int32, (SEGS, WIDE), 0) == 0
    for j in range(3):
        nat = pltpu.roll(swapped(inter[pl.ds(8 * (steps + j), 8), :], flips), 1, 0)
        nat = jnp.where(first, edge[5 + j : 6 + j, :], nat)
        inter[8 * j : 8 * j + 8, :] = swapped(nat, flips)

    def tile(i, carry):
        prod, state = carry
        base = pl.multiple_of(i * TILE, TILE)
        c = code[pl.ds(base, TILE), :]
        v = small[0:1, :] * inter[pl.ds(base + 24, TILE), :]
        for k in (1, 2, 3):
            v = v + jnp.where(
                c >= k, small[k : k + 1, :] * inter[pl.ds(base + 24 - 8 * k, TILE), :], 0.0
            )
        high = v.astype(jnp.bfloat16)
        low = (v - high.astype(jnp.float32)).astype(jnp.bfloat16)
        mat = gates[0]
        pre = jnp.dot(
            jnp.concatenate([high, low], axis=1),
            jnp.concatenate([mat, mat], axis=0),
            preferred_element_type=jnp.float32,
        )
        rg = 1.0 / (1.0 + jnp.exp(-(pre[:, :WIDE] + small[5:6, :])))
        ig = jax.nn.sigmoid(pre[:, WIDE:] + small[6:7, :])
        la = small[4:5, :] * rg
        e = jnp.exp(la)
        sq = jnp.sqrt(jnp.tanh(-la) * (1.0 + e * e))
        here = pl.ds(base, TILE)
        v_out[here, :] = v
        rg_out[here, :] = rg
        ig_out[here, :] = ig
        e_out[here, :] = e
        sq_out[here, :] = sq
        keep = jnp.where(c > 0, e, 0.0)
        inflow = sq * ig * v
        for s in range(TILE // SEGS):
            k = keep[8 * s : 8 * s + 8]
            prod = prod * k
            state = k * state + inflow[8 * s : 8 * s + 8]
        return prod, state

    prod, state = lax.fori_loop(
        0,
        rows // TILE,
        tile,
        (jnp.ones((SEGS, WIDE), jnp.float32), jnp.zeros((SEGS, WIDE), jnp.float32)),
    )
    coef, base, whole = exclusive(prod, state, flips, False)
    maps[0:8, :] = prod
    maps[8:16, :] = coef
    maps[16:24, :] = base
    total[...] = whole


def state_kernel(count, parts, where, v, ig, e, sq, code, maps, *rest):
    others, p_parts = rest[: count - 1], rest[count - 1 : count - 1 + parts]
    hs, out, wide, p = rest[count - 1 + parts :]
    lay_out(p_parts, p)
    rows = v.shape[0]
    steps = rows // SEGS
    mine = where[1]
    entry = jnp.zeros((1, WIDE), jnp.float32)
    for d in range(count - 1, 0, -1):
        piece = others[d - 1]
        entry = jnp.where(mine >= d, piece[0:1, :] * entry + piece[1:2, :], entry)
    state = maps[8:16, :] * entry + maps[16:24, :]
    hs[0:8, :] = state

    def tile(i, state):
        base = pl.multiple_of(i * TILE, TILE)
        here = pl.ds(base, TILE)
        keep = jnp.where(code[here, :] > 0, e[here, :], 0.0)
        inflow = sq[here, :] * ig[here, :] * v[here, :]
        for s in range(TILE // SEGS):
            state = keep[8 * s : 8 * s + 8] * state + inflow[8 * s : 8 * s + 8]
            hs[pl.ds(base + 8 * s + 8, 8), :] = state
            there = pl.ds(i * (TILE // SEGS) + s, 8, stride=steps)
            wide[there, :] = state * gelu_only(p[there, :])
        return state

    lax.fori_loop(0, rows // TILE, tile, state)
    out[...] = wide[...].astype(jnp.bfloat16)


def adjoint_kernel(parts, p_count, where, hs, e, code, maps, *rest):
    dhs, dp, back, total, wide, do, p = rest[parts + p_count :]
    lay_out(rest[:parts], do)
    lay_out(rest[parts : parts + p_count], p)
    rows = do.shape[0]
    steps = rows // SEGS
    flips = where[0]

    def tile(i, grad):
        i = rows // TILE - 1 - i
        base = pl.multiple_of(i * TILE, TILE)
        keep = jnp.where(code[pl.ds(base, TILE), :] > 0, e[pl.ds(base, TILE), :], 0.0)
        for s in range(TILE // SEGS - 1, -1, -1):
            there = pl.ds(i * (TILE // SEGS) + s, 8, stride=steps)
            d = do[there, :]
            act, slope = gelu_pair(p[there, :])
            wide[there, :] = d * hs[pl.ds(base + 8 * s + 8, 8), :] * slope
            dh = d * act
            dhs[pl.ds(base + 8 * s, 8), :] = dh
            grad = keep[8 * s : 8 * s + 8] * (dh + grad)
        return grad

    grad = lax.fori_loop(0, rows // TILE, tile, jnp.zeros((SEGS, WIDE), jnp.float32))
    dp[...] = wide[...].astype(jnp.bfloat16)
    coef, base, whole = exclusive(maps[0:8, :], grad, flips, True)
    back[0:8, :] = coef
    back[8:16, :] = base
    total[...] = whole


def leave_kernel(count, where, dhs, inter, v, rg, ig, e, sq, hs, code, small, gates_t, back, *rest):
    products, grads = rest[: count - 1], rest[count - 1 : 2 * count - 2]
    du, grad_gates, sums, edge, dv_all, wide = rest[2 * count - 1 :]
    rows = dhs.shape[0]
    steps = rows // SEGS
    flips, mine = where[0], where[1]
    entry = jnp.zeros((1, WIDE), jnp.float32)
    for j in range(count - 1, 0, -1):
        d = count - j
        entry = jnp.where(
            mine + j < count, products[d - 1][0:1, :] * entry + grads[d - 1][1:2, :], entry
        )
    grad = back[0:8, :] * entry + back[8:16, :]
    grad_gates[...] = jnp.zeros_like(grad_gates)

    def fold(x):
        parts = [x[8 * s : 8 * s + 8] for s in range(TILE // SEGS)]
        while len(parts) > 1:
            parts = [a + b for a, b in zip(parts[::2], parts[1::2])]
        return parts[0]

    def tile(i, carry):
        grad, taps, decay, shift_a, shift_i = carry
        i = rows // TILE - 1 - i
        base = pl.multiple_of(i * TILE, TILE)
        here = pl.ds(base, TILE)
        c = code[here, :]
        e_now, sq_now, rg_now, ig_now, v_now = e[here, :], sq[here, :], rg[here, :], ig[here, :], v[here, :]
        keep = jnp.where(c > 0, e_now, 0.0)
        d_now = dhs[here, :]
        pieces = [None] * (TILE // SEGS)
        for s in range(TILE // SEGS - 1, -1, -1):
            a = d_now[8 * s : 8 * s + 8] + grad
            pieces[s] = a
            grad = keep[8 * s : 8 * s + 8] * a
        a = jnp.concatenate(pieces, axis=0)
        q = ig_now * v_now
        dla = a * (keep * hs[here, :] - q * (e_now * e_now) / jnp.maximum(sq_now, 1e-25))
        rate = rg_now * dla
        decay = decay + fold(rate)
        dra = small[4:5, :] * rate * (1.0 - rg_now)
        asq = a * sq_now
        dia = asq * q * (1.0 - ig_now)
        shift_a = shift_a + fold(dra)
        shift_i = shift_i + fold(dia)
        both = jnp.concatenate([dra.astype(jnp.bfloat16), dia.astype(jnp.bfloat16)], axis=1)
        dv = asq * ig_now + jnp.dot(both, gates_t[0], preferred_element_type=jnp.float32)
        grad_gates[0] += lax.dot_general(
            v_now.astype(jnp.bfloat16),
            both,
            (((0,), (0,)), ((), ())),
            preferred_element_type=jnp.float32,
        )
        dv_all[here, :] = dv
        new_taps = [taps[0] + fold(dv * inter[pl.ds(base + 24, TILE), :])]
        for k in (1, 2, 3):
            new_taps.append(
                taps[k]
                + fold(jnp.where(c >= k, dv * inter[pl.ds(base + 24 - 8 * k, TILE), :], 0.0))
            )
        return grad, tuple(new_taps), decay, shift_a, shift_i

    zero = jnp.zeros((SEGS, WIDE), jnp.float32)
    _, taps, decay, shift_a, shift_i = lax.fori_loop(
        0, rows // TILE, tile, (grad, (zero,) * 4, zero, zero, zero), unroll=2
    )
    totals = [jnp.sum(x, axis=0, keepdims=True) for x in (*taps, decay, shift_a, shift_i)]
    sums[...] = jnp.concatenate(totals + [jnp.zeros((1, WIDE), jnp.float32)], axis=0)
    last = lax.broadcasted_iota(jnp.int32, (SEGS, WIDE), 0) == SEGS - 1
    edges = []
    for j in range(3):
        nat = swapped(dv_all[8 * j : 8 * j + 8, :], flips)
        edges.append(nat[0:1])
        nat = jnp.where(last, 0.0, pltpu.roll(nat, SEGS - 1, 0))
        dv_all[pl.ds(rows + 8 * j, 8), :] = swapped(nat, flips)
    edge[...] = jnp.concatenate(edges + [jnp.zeros((SEGS - 3, WIDE), jnp.float32)], axis=0)

    def mix(i, carry):
        base = pl.multiple_of(i * TILE, TILE)
        total = small[0:1, :] * dv_all[pl.ds(base, TILE), :]
        for k in (1, 2, 3):
            there = pl.ds(base + 8 * k, TILE)
            total = total + jnp.where(
                code[there, :] >= k, small[k : k + 1, :] * dv_all[there, :], 0.0
            )
        for s in range(TILE // SEGS):
            wide[pl.ds(i * (TILE // SEGS) + s, 8, stride=steps), :] = total[8 * s : 8 * s + 8]
        return carry

    lax.fori_loop(0, rows // TILE, mix, 0)
    du[...] = wide[...].astype(jnp.bfloat16)


def copy_kernel(pick, x, out):
    out[...] = x[0, 0]


def reordered(pick, x, name):
    _, segs, rows, width = x.shape
    return pl.pallas_call(
        copy_kernel,
        grid_spec=pltpu.PrefetchScalarGridSpec(
            num_scalar_prefetch=1,
            grid=(segs,),
            in_specs=[pl.BlockSpec((1, 1, rows, width), lambda s, p: (p[1], s ^ p[0], 0, 0))],
            out_specs=pl.BlockSpec((rows, width), lambda s, p: (s, 0)),
        ),
        out_shape=jax.ShapeDtypeStruct((segs * rows, width), x.dtype),
        cost_estimate=cost(0.3),
        name=name,
    )(pick, x)


def nt(left_mat, right_mat):
    return lax.dot_general(
        left_mat, right_mat, (((1,), (1,)), ((), ())), preferred_element_type=jnp.float32
    )


def cost(us):
    return pl.CostEstimate(flops=int(us * 1e9), bytes_accessed=1, transcendentals=0)


def nt(left_mat, right_mat):
    return lax.dot_general(
        left_mat, right_mat, (((1,), (1,)), ((), ())), preferred_element_type=jnp.float32
    )


def mlp_kernel(h, dy, wg, wu, wd, mid, low_gate, low_up, part):
    up_pre = nt(h[...], wu[...])
    act, slope = gelu_pair(nt(h[...], wg[...]))
    grad_mid = nt(dy[...], wd[...])
    mid[...] = (act * up_pre).astype(jnp.bfloat16)
    low_gate[...] = (grad_mid * (up_pre * slope)).astype(jnp.bfloat16)
    low_up[...] = (grad_mid * act).astype(jnp.bfloat16)
    part[...] = (
        jnp.dot(low_gate[...], wg[...], preferred_element_type=jnp.float32)
        + jnp.dot(low_up[...], wu[...], preferred_element_type=jnp.float32)
    ).astype(part.dtype)


def mlp(h, cot, block, wg, wu, wd, kind):
    rows, width = h.shape
    hidden = wg.shape[0]
    step = min(rows, 256)
    count = rows // step
    row_spec = pl.BlockSpec((step, width), lambda j: (j, 0))
    cot_spec = pl.BlockSpec((step, width), lambda j: (j + block * count, 0))
    weight = pl.BlockSpec((hidden, width), lambda j: (0, 0))
    act = pl.BlockSpec((step, hidden), lambda j: (j, 0))
    low_shape = jax.ShapeDtypeStruct((rows, hidden), jnp.bfloat16)
    wg, wu, wd = (pltpu.with_memory_space_constraint(w, pltpu.VMEM) for w in (wg, wu, wd))
    return pl.pallas_call(
        mlp_kernel,
        grid=(count,),
        in_specs=[row_spec, cot_spec, weight, weight, weight],
        out_specs=[act, act, act, row_spec],
        out_shape=[low_shape] * 3 + [jax.ShapeDtypeStruct((rows, width), kind)],
        compiler_params=pltpu.CompilerParams(vmem_limit_bytes=24 * 2**20),
        cost_estimate=cost(0.3),
        name="mlp",
    )(h, cot, wg, wu, wd)


CHUNK = 192


def grads_kernel(spans, lefts, which, cuts, added, *refs):
    rights = [refs[lefts + i] for i in which]
    more = refs[lefts + max(which) + 1 :][:added]
    outs = refs[lefts + max(which) + 1 + added :]
    count, _, part = outs[0].shape
    at = 0
    for left, right, (low_col, high_col) in zip(refs[:lefts], rights, spans):
        first = low_col // WIDE * WIDE
        last = min(-(-high_col // WIDE) * WIDE, left.shape[1])
        total = lax.dot_general(
            left[:, first:last],
            right[...],
            (((0,), (0,)), ((), ())),
            preferred_element_type=jnp.float32,
        )
        done = 0
        while done < high_col - low_col:
            size = min(cuts, high_col - low_col - done)
            rows = low_col - first + done
            for z in range(count):
                piece = total[rows : rows + size, z * part : (z + 1) * part]
                if added:
                    piece = piece + more[at // cuts][z].astype(jnp.float32)
                if len(outs) > 1:
                    outs[at // cuts][z] = piece.astype(jnp.bfloat16)
                else:
                    outs[0][z, at : at + size, :] = piece.astype(jnp.bfloat16)
            done += size
            at += size


def grads(pairs, half, halves, count, split=False, added=()):
    spans, rows = [], 0
    for left, _ in pairs:
        size = left.shape[1] // halves
        spans.append((half * size, (half + 1) * size))
        rows += size
    part = pairs[0][1].shape[1] // count
    sizes = [b - a for a, b in spans]
    cuts = rows if len(sizes) == 1 else 16
    if split or added:
        cuts = next(c for c in (CHUNK, 128, 64, 16) if all(s % c == 0 for s in sizes))
    rights, which = [], []
    for _, right in pairs:
        if not any(right is r for r in rights):
            rights.append(right)
        which.append(next(i for i, r in enumerate(rights) if r is right))
    args = [p[0] for p in pairs] + rights + list(added)
    shape = (count, cuts if split else rows, part)
    return pl.pallas_call(
        functools.partial(grads_kernel, spans, len(pairs), which, cuts, len(added)),
        out_shape=[jax.ShapeDtypeStruct(shape, jnp.bfloat16)] * (rows // cuts if split else 1),
        compiler_params=pltpu.CompilerParams(vmem_limit_bytes=32 * 2**20),
        cost_estimate=cost(0.3),
        name="grads",
    )(*args)


def lanes(rows, offset=0):
    return pl.BlockSpec((rows, WIDE), lambda n: (0, n + offset))


def paths(rows, groups, halves, offset):
    size = groups // halves
    return pl.BlockSpec((rows, WIDE), lambda n: (0, n + (n // size + offset) * size))


def per_block(shape):
    return pl.BlockSpec((1,) + shape, lambda n: (n, 0, 0))


def scalars():
    return pl.BlockSpec(memory_space=pltpu.SMEM)


def shared(shape):
    return pl.BlockSpec(shape, lambda n: (0,) * len(shape))


def launch(kernel, groups, in_specs, outs, scratch, args, name, aliases={}):
    def place(shape, dtype):
        if shape[0] >= 512 and (dtype == jnp.float32 or shape[1] == 2 * groups * WIDE):
            return pltpu.HBM(shape, dtype)
        return jax.ShapeDtypeStruct(shape, dtype)

    def pin(a):
        if a.shape[0] >= 512 and (
            a.dtype == jnp.float32 or a.shape[1] == 2 * groups * WIDE
        ):
            return pltpu.with_memory_space_constraint(a, pltpu.HBM)
        return a

    return pl.pallas_call(
        kernel,
        grid=(groups,),
        in_specs=in_specs,
        out_specs=[spec for _, _, spec in outs],
        out_shape=[place(shape, dtype) for shape, dtype, _ in outs],
        scratch_shapes=scratch,
        compiler_params=pltpu.CompilerParams(vmem_limit_bytes=16 * 2**20),
        cost_estimate=cost(0.3),
        name=name,
        input_output_aliases=aliases,
    )(*[pin(a) for a in args])


def enter(where, both, edge, code, small, gates, halves):
    parts, size = len(both), both[0].shape[0]
    rows, channels = parts * size, both[0].shape[1] // 2
    groups = channels // WIDE
    f32 = jnp.float32
    full = ((rows, channels), f32, lanes(rows))
    return launch(
        functools.partial(enter_kernel, parts),
        groups,
        [
            scalars(),
            paths(8, groups, halves, 0),
            shared(code.shape),
            lanes(8),
            per_block((WIDE, 2 * WIDE)),
        ]
        + [paths(size, groups, halves, 0)] * parts,
        [
            ((rows + 24, channels), f32, lanes(rows + 24)),
            full,
            full,
            full,
            full,
            full,
            ((24, channels), f32, lanes(24)),
            ((8, channels), f32, lanes(8)),
        ],
        [pltpu.VMEM((rows, WIDE), f32)],
        (where, edge, code, small, gates, *both),
        "enter",
    )


def states_of(where, v, ig, e, sq, code, both, maps, others, halves):
    rows, channels = v.shape
    parts, size = len(both), both[0].shape[0]
    groups = channels // WIDE
    f32 = jnp.float32
    return launch(
        functools.partial(state_kernel, len(others) + 1, parts),
        groups,
        [scalars()]
        + [lanes(rows)] * 4
        + [shared(code.shape), lanes(24)]
        + [lanes(8)] * len(others)
        + [paths(size, groups, halves, 1)] * parts,
        [
            ((rows + 8, channels), f32, lanes(rows + 8)),
            ((rows, channels), jnp.bfloat16, lanes(rows)),
        ],
        [pltpu.VMEM((rows, WIDE), f32)] * 2,
        (where, v, ig, e, sq, code, maps, *others, *both),
        "states",
    )


def adjoints(where, do, both, hs, e, code, maps, halves):
    parts, (size, channels) = len(do), do[0].shape
    p_count, p_size = len(both), both[0].shape[0]
    rows = parts * size
    groups = channels // WIDE
    f32 = jnp.float32
    return launch(
        functools.partial(adjoint_kernel, parts, p_count),
        groups,
        [scalars(), lanes(rows + 8), lanes(rows), shared(code.shape), lanes(24)]
        + [lanes(size)] * parts
        + [paths(p_size, groups, halves, 1)] * p_count,
        [
            ((rows, channels), f32, lanes(rows)),
            ((rows, 2 * channels), jnp.bfloat16, paths(rows, groups, halves, 1)),
            ((16, channels), f32, lanes(16)),
            ((8, channels), f32, lanes(8)),
        ],
        [pltpu.VMEM((rows, WIDE), f32)] * 3,
        (where, hs, e, code, maps, *do, *both),
        "adjoint",
    )


def leave(where, dhs, kept, hs, code, small, gates_t, back, products, grads, half_done, halves):
    inter, v, rg, ig, e, sq = kept
    rows, channels = dhs.shape
    groups = channels // WIDE
    f32 = jnp.float32
    count = len(products) + 1
    return launch(
        functools.partial(leave_kernel, count),
        groups,
        [scalars(), lanes(rows), lanes(rows + 24)]
        + [lanes(rows)] * 5
        + [
            lanes(rows + 8),
            shared(code.shape),
            lanes(8),
            per_block((2 * WIDE, WIDE)),
            lanes(16),
        ]
        + [lanes(8)] * (2 * count - 2)
        + [pl.BlockSpec(memory_space=pl.ANY)],
        [
            ((rows, 2 * channels), jnp.bfloat16, paths(rows, groups, halves, 0)),
            ((groups, WIDE, 2 * WIDE), f32, per_block((WIDE, 2 * WIDE))),
            ((8, channels), f32, lanes(8)),
            ((8, channels), f32, lanes(8)),
        ],
        [pltpu.VMEM((rows + 24, WIDE), f32), pltpu.VMEM((rows, WIDE), f32)],
        (where, dhs, inter, v, rg, ig, e, sq, hs, code, small, gates_t, back, *products, *grads, half_done),
        "leave",
        {11 + 2 * count: 0},
    )


def dense(left_mat, right_mat):
    return jnp.dot(left_mat, right_mat, preferred_element_type=jnp.float32)


def dense_nt(left_mat, right_mat):
    return lax.dot_general(
        left_mat, right_mat, (((1,), (1,)), ((), ())), preferred_element_type=jnp.float32
    )


def dense_tn(left_mat, right_mat):
    return lax.dot_general(
        left_mat, right_mat, (((0,), (0,)), ((), ())), preferred_element_type=jnp.float32
    )


def low(x):
    return x.astype(jnp.bfloat16)


def high(x):
    return x.astype(jnp.float32)


def after(x, *others):
    return lax.optimization_barrier((x,) + others)[0]


def tied(*values):
    return lax.optimization_barrier(values)


def turned(x, axis, distance):
    count = lax.axis_size(axis)
    return lax.ppermute(x, axis, [(i, (i + distance) % count) for i in range(count)])


def around(x, axis):
    return [turned(x, axis, d) for d in range(1, lax.axis_size(axis))]


def in_order(x, pieces, axis):
    count = lax.axis_size(axis)
    mine = lax.axis_index(axis)
    turn = jnp.stack([x] + pieces[::-1])
    turn = jnp.concatenate([turn, turn], axis=0)
    return lax.dynamic_slice_in_dim(turn, (count - mine) % count, count, 0)


def flip(x, bits):
    count = lax.axis_size("mp")
    return lax.ppermute(x, "mp", [(i, i ^ bits) for i in range(count)])


class Paired:
    halves = 2
    blocks = 4

    def spread(self, rows):
        half = rows.shape[0] // 2
        a, b = rows[:half], rows[half:]
        xb, ya = flip(b, 2), flip(a, 4)
        xa, yb = flip(a, 2), flip(b, 4)
        da, db = flip(ya, 2), flip(xb, 4)
        pairs = ((xa, xb), (ya, yb), (da, db))
        return [rows] + [jnp.concatenate(p, axis=0) for p in pairs], (da, db)

    def give(self, part, block):
        return part if block == 0 else flip(part, 2 * block)

    def gather_sum(self, pieces):
        total = high(pieces[0])
        for piece in pieces[1:]:
            total = total + high(piece)
        return total

    def collect(self, part):
        p3 = low(part(3))
        half = p3.shape[0] // 2
        r2a, r1b = flip(p3[:half], 2), flip(p3[half:], 4)
        p1, p2 = part(1), part(2)
        s1a, s2b = flip(low(p1[:half]), 2), flip(low(p2[half:]), 4)
        p0 = part(0)
        s2a = flip(low(high(p2[:half]) + high(r2a)), 4)
        s1b = flip(low(high(p1[half:]) + high(r1b)), 2)
        return (p0, s1a, s1b, s2a, s2b), (r2a, r1b)

    def finish(self, pieces):
        p0, s1a, s1b, s2a, s2b = pieces
        far = [
            jnp.concatenate([s1a, s1b], axis=0),
            jnp.concatenate([s2a, s2b], axis=0),
        ]
        return high(p0) + high(far[0]) + high(far[1])

    def both(self, x):
        return [x, flip(x, 1)]

    def sent_totals(self, pairs, count):
        return [flip(x, 1) for x in grads(pairs, 1, 2, count, split=True)]

    def own_totals(self, pairs, count, sent):
        return grads(pairs, 0, 2, count, added=sent)[0]

    def owner_small(self, grad_gates, lines, gains):
        blocks, channels = grad_gates.shape[0] // 2, lines.shape[1] // 2
        grad_gates = grad_gates[:blocks] + flip(grad_gates[blocks:], 1)
        lines = lines[:, :channels] + flip(lines[:, channels:], 1)
        return small_sums(grad_gates, lines, gains)

    def plane_sum(self, gains):
        for bits in (1, 2, 4):
            gains = gains + flip(gains, bits)
        return gains


class Plain:
    halves = 1
    blocks = 1

    def spread(self, rows):
        rows = lax.all_gather(rows, "mp", axis=0, tiled=True)
        return [rows], (rows,)

    def collect(self, part):
        rows = lax.psum_scatter(low(part(0)), "mp", scatter_dimension=0, tiled=True)
        return (rows,), (rows,)

    def finish(self, pieces):
        return high(pieces[0])

    def both(self, x):
        return [x]

    def sent_totals(self, pairs, count):
        return []

    def own_totals(self, pairs, count, sent):
        return grads(pairs, 0, 1, count)[0]

    def owner_small(self, grad_gates, lines, gains):
        return small_sums(grad_gates, lines, gains)

    def plane_sum(self, gains):
        return lax.psum(gains, "mp")


def small_sums(grad_gates, lines, gains):
    count, seq_rank = lax.axis_size("seq"), lax.axis_index("seq")
    blocks = grad_gates.shape[0]
    depth, thin, part = WIDE // count, lines.shape[1] // count, gains.shape[1] // count
    pieces = jnp.concatenate(
        [
            grad_gates.reshape(blocks, count, depth, 2 * WIDE).transpose(1, 0, 2, 3).reshape(count, -1),
            lines.reshape(-1, count, thin).transpose(1, 0, 2).reshape(count, -1),
            gains.reshape(2, count, part).transpose(1, 0, 2).reshape(count, -1),
        ],
        axis=1,
    )
    size = pieces.shape[1]
    pieces = jnp.pad(pieces, ((0, 0), (0, -size % 1024))).reshape(count, -1, WIDE)
    total = lax.dynamic_index_in_dim(pieces, seq_rank, 0, keepdims=False)
    for d in range(1, count):
        piece = lax.dynamic_index_in_dim(pieces, (seq_rank + d) % count, 0, keepdims=False)
        total = total + turned(piece, "seq", d)
    total = total.reshape(-1)
    at = blocks * depth * 2 * WIDE
    sum_gates = total[:at].reshape(blocks, depth, 2, WIDE)
    lines = total[at : at + 7 * thin].reshape(7, thin)
    at += 7 * thin
    return sum_gates, lines, total[at : at + 2 * part].reshape(2, part)


def mask_code(starts_row, first_pos, flips, steps):
    shape = ((steps + 3) * SEGS, WIDE)
    row = lax.broadcasted_iota(jnp.int32, shape, 0)
    places = first_pos + ((row & (SEGS - 1)) ^ flips) * steps + (row // SEGS)
    code = jnp.full(shape, 4, jnp.int32)
    for e in range(starts_row.shape[0]):
        away = places - starts_row[e]
        code = jnp.where((starts_row[e] > 0) & (away >= 0), jnp.minimum(code, away), code)
    return code.astype(jnp.float32)


def normed(rows):
    scale = lax.rsqrt(jnp.mean(rows * rows, axis=-1, keepdims=True) + epsilon)
    return rows * scale, scale


def norm_back(grad_norm, norm, scale):
    return scale * (grad_norm - norm * jnp.mean(grad_norm * norm, axis=-1, keepdims=True))


def small_weights(gate_a, gate_i, conv_w, decay_param, bias_a, bias_i, gain_one, gain_two):
    blocks, depth, _ = gate_a.shape
    taps, thin = conv_w.shape
    part = gain_one.shape[0]
    count = lax.axis_size("seq")
    if part % WIDE == 0 and thin <= WIDE:
        lines = jnp.concatenate([conv_w, decay_param[None], bias_a[None], bias_i[None]], axis=0)
        lines = jnp.pad(lines, ((0, 1), (0, WIDE - thin)))
        gains = jnp.concatenate([gain_one.reshape(-1, WIDE), gain_two.reshape(-1, WIDE)], axis=0)
        pack = jnp.concatenate(
            [gate_a.reshape(-1, WIDE), gate_i.reshape(-1, WIDE), lines, gains], axis=0
        )
        pack = jnp.pad(pack, ((0, -pack.shape[0] % 16), (0, 0)))
        pack = in_order(pack, around(pack, "seq"), "seq")
        at = blocks * depth
        ga, gi = (
            pack[:, i * at : (i + 1) * at].reshape(count, blocks, depth, WIDE).transpose(1, 0, 2, 3)
            for i in (0, 1)
        )
        ga, gi = (x.reshape(blocks, count * depth, WIDE) for x in (ga, gi))
        lines = pack[:, 2 * at : 2 * at + taps + 3, :thin].transpose(1, 0, 2).reshape(taps + 3, -1)
        at = 2 * at + taps + 4
        size = part // WIDE
        gain_one = pack[:, at : at + size].reshape(-1)
        gain_two = pack[:, at + size : at + 2 * size].reshape(-1)
    else:
        ga, gi = (lax.all_gather(x, "seq", axis=1, tiled=True) for x in (gate_a, gate_i))
        lines = jnp.concatenate([conv_w, decay_param[None], bias_a[None], bias_i[None]], axis=0)
        lines = lax.all_gather(lines, "seq", axis=1, tiled=True)
        gain_one, gain_two = (
            lax.all_gather(x, "seq", axis=0, tiled=True) for x in (gain_one, gain_two)
        )
    return jnp.concatenate([ga, gi], axis=2), high(lines), high(gain_one), high(gain_two)


def micro(plan, where, flips, stream, cot, starts_row, weights):
    first, pack, smalls = weights
    count = stream.shape[0] * lax.axis_size("mp") // plan.halves
    steps = count // SEGS
    size = count // plan.blocks
    blocks_of_z = lax.axis_size("seq")
    seq_rank = lax.axis_index("seq")
    wide = plan.halves
    def rows_of(x, b):
        return x[b * size : (b + 1) * size]

    n1, s1 = normed(stream)
    low_n1 = low(n1)
    h1, _ = plan.spread(low_n1)
    second = lax.all_gather(pack, "seq", axis=1, tiled=True)
    come = h1[min(1, plan.blocks - 1)]
    starts_row = after(starts_row, come)
    code = mask_code(starts_row, seq_rank * count, flips, steps)
    gates, lines, gain_one, gain_two = small_weights(*after(smalls, come))
    gates = jnp.concatenate(plan.both(gates), axis=0)
    lines = jnp.concatenate(plan.both(lines), axis=1)
    taps, decay = lines[:4], lines[4]
    channels = lines.shape[1]
    own = channels // wide
    rate = -8.0 * jax.nn.softplus(decay)
    small = jnp.concatenate([taps, rate[None], lines[5:7], jnp.zeros((1, channels))], axis=0)
    gates_t = jnp.concatenate(
        [gates[:, :, :WIDE].transpose(0, 2, 1), gates[:, :, WIDE:].transpose(0, 2, 1)], axis=1
    )
    h1 = jnp.concatenate([low(high(h) * gain_one) for h in h1], axis=0)
    other = plan.both(after(first, h1, code, small, gates, gates_t, pack))
    wxy = jnp.concatenate([x[i] for x in other for i in (0, 1)], axis=0)
    wo = jnp.concatenate([x[2] for x in other], axis=0)
    up_both = [dense_nt(rows_of(h1, b), wxy) for b in range(plan.blocks)]
    last = lax.dynamic_slice_in_dim(h1, ((SEGS - 1) ^ flips) * steps + steps - 8, 8, 0)
    before = turned(last, "seq", 1)
    edge = jnp.where(seq_rank > 0, dense_nt(before, wxy), 0.0)
    *kept, maps, total = enter(where, up_both, edge, code, small, gates, wide)
    inter, v, rg, ig, e, sq = kept
    fore = around(total, "seq")
    hs, mixed = states_of(where, v, ig, e, sq, code, up_both, maps, fore, wide)

    more, come = plan.collect(lambda b: dense(rows_of(mixed, b), wo))
    cot = cot(come[0])
    middle = stream + plan.finish(after(more, cot))
    n2, s2 = normed(middle)
    h2, come = plan.spread(low(n2 * gain_two))
    second = after(second, *come)
    third = second.shape[0] // 3
    wg, wu, wd = (
        jnp.concatenate(plan.both(second[i * third : (i + 1) * third]), axis=0) for i in range(3)
    )
    each = range(plan.blocks)
    found = {}
    for b in list(each)[::-1]:
        kind = jnp.float32 if b == 0 and plan.blocks > 1 else jnp.bfloat16
        found[b] = mlp(h2[b], cot, b, wg, wu, wd, kind)
    back_two, come = plan.collect(lambda b: found[b][3])
    mid, low_gate, low_up = (
        jnp.concatenate([found[b][i] for b in each], axis=0) for i in (0, 1, 2)
    )
    h2 = jnp.concatenate(h2, axis=0)
    mid = after(mid, *come)
    low_gate = after(low_gate, *back_two[1:])
    sent_wd = plan.sent_totals([(mid, cot)], blocks_of_z)
    pack_wd = plan.own_totals([(mid, cot)], blocks_of_z, sent_wd)
    grad_wd = owner_sum(pack_wd)
    pairs = [(low_gate, h2), (low_up, h2)]
    sent_gate_up = plan.sent_totals(pairs, blocks_of_z)
    back_two = plan.finish(after(back_two, pack_wd, *sent_gate_up))
    grad_two = jnp.sum(back_two * n2, axis=0)
    grad_middle = high(cot_rows_of(plan, cot, stream.shape[0])) + norm_back(
        back_two * gain_two, n2, s2
    )
    low_middle = low(grad_middle)
    mid_rows, _ = plan.spread(low_middle)
    pairs = [(after(low_gate, low_middle), h2), (low_up, h2)]
    pack_gate_up = plan.own_totals(pairs, blocks_of_z, sent_gate_up)
    grad_gate_up = owner_sum(pack_gate_up)
    shares = dense(after(mid, pack_gate_up), wd)
    shares = [rows_of(shares, b) for b in each]
    shares = [x if b == 0 else low(x) for b, x in enumerate(shares)]
    mid_rows = after(jnp.concatenate(mid_rows, axis=0), *shares)
    do = [dense_nt(mid_rows, wo)]
    block_parts, _ = plan.collect(lambda b: after(shares[b], do[0]))
    dhs, dup, back, total = adjoints(where, do, up_both, hs, e, code, maps, wide)
    aft = around(total, "seq")
    dhs, grad_wd = tied(dhs, grad_wd)
    dup, grad_gates, sums, edge = leave(
        where, dhs, kept, hs, code, small, gates_t, back, fore, aft, dup, wide
    )
    nxt = jnp.where(seq_rank < lax.axis_size("seq") - 1, turned(edge, "seq", -1), 0.0)
    spots = [(steps + j) * SEGS + ((SEGS - 1) ^ flips) for j in range(3)]
    far = jnp.concatenate([lax.dynamic_slice(code, (i, 0), (1, 1)) for i in spots], axis=0)
    extra = [jnp.zeros((5, channels))]
    for j in range(3):
        row = jnp.zeros((1, channels))
        for k in range(3 - j, 4):
            i = j + k - 3
            row = row + jnp.where(far[i : i + 1] >= k, taps[k : k + 1] * nxt[i : i + 1], 0.0)
        extra.append(row)
    extra = jnp.concatenate(extra, axis=0)
    at = ((SEGS - 1) ^ flips) * steps + steps - 8
    extra = low(interleaved(extra, jnp.zeros_like(extra), wide))
    patch = low(high(lax.dynamic_slice_in_dim(dup, at, 8, 0)) + high(extra))
    dup = lax.dynamic_update_slice_in_dim(dup, patch, at, 0)
    pairs = [(dup, h1), (mixed, mid_rows)]
    pack_late = plan.own_totals(pairs, blocks_of_z, plan.sent_totals(pairs, blocks_of_z))
    dup, pack_late = tied(dup, pack_late)
    parts = {b: dense(rows_of(dup, b), wxy) for b in list(each)[::-1]}
    back_one, _ = plan.collect(lambda b: parts[b])
    grad_one = sum(jnp.sum(parts[b] * high(rows_of(h1, b)), axis=0) for b in parts) / gain_one
    pack_late, grad_gate_up = tied(pack_late, grad_gate_up)
    late = owner_sum(pack_late)
    decay_sum = -8.0 * jax.nn.sigmoid(decay) * sums[4]
    lines = jnp.concatenate([sums[:4], decay_sum[None], sums[5:7]], axis=0)
    little = plan.owner_small(grad_gates, lines, jnp.stack([grad_one, grad_two]))
    back_one = plan.finish(back_one)
    grad_rows = low(grad_middle + norm_back(back_one * gain_one, n1, s1))
    block_rows = low(middle + plan.finish(after(block_parts, little[2])))
    little = little[:2] + (plan.plane_sum(after(little[2], grad_rows)),)
    large = tuple(high(x) for x in (late, grad_gate_up, grad_wd))
    return block_rows, grad_rows, large, little


def interleaved(first, second, halves):
    size = first.shape[1] // halves
    return jnp.concatenate(
        [x[:, i * size : (i + 1) * size] for i in range(halves) for x in (first, second)], axis=1
    )


def cot_rows_of(plan, cot, rows):
    if plan.halves == 2:
        return cot[:rows]
    return lax.dynamic_slice_in_dim(cot, lax.axis_index("mp") * rows, rows, 0)


def owner_sum(pack):
    return lax.psum_scatter(pack, "seq", scatter_dimension=0, tiled=False)


def on_device(
    tokens,
    cotangent,
    w_x,
    w_y,
    w_out,
    w_gate,
    w_up,
    w_down,
    gate_a,
    gate_i,
    conv_w,
    decay_param,
    bias_a,
    bias_i,
    gain_one,
    gain_two,
    doc_starts,
):
    micros, own_rows, _ = tokens.shape
    span = cotangent.shape[1]
    count = lax.axis_size("seq")
    seq_rank = lax.axis_index("seq")
    mp_rank = lax.axis_index("mp")
    paired = micros == 2 and lax.axis_size("mp") == SEGS and span == SEGS * own_rows
    plan = Paired() if paired else Plain()
    channels, hidden = w_x.shape[1], w_gate.shape[1]
    blocks, depth, _ = gate_a.shape
    part = w_x.shape[0]
    thin = conv_w.shape[1]

    first = lax.all_gather(
        jnp.stack([w_x.T, w_y.T, w_out]), "seq", axis=2, tiled=True
    )
    second = lax.optimization_barrier(jnp.concatenate([w_gate.T, w_up.T, w_down], axis=0))
    smalls = (gate_a, gate_i, conv_w, decay_param, bias_a, bias_i, gain_one, gain_two)
    weights = (first, second, smalls)

    if paired:
        core = mp_rank % 2
        mine = lax.dynamic_index_in_dim(tokens, core, 0, keepdims=False)
        other = flip(lax.dynamic_index_in_dim(tokens, 1 - core, 0, keepdims=False), 1)
        stream = high(jnp.concatenate([mine, other], axis=0))
        pick = jnp.stack([mp_rank, core]).astype(jnp.int32)
        folded = cotangent.reshape(micros, SEGS, own_rows, -1)
        where = jnp.stack([mp_rank, seq_rank]).astype(jnp.int32)
        starts_row = lax.dynamic_index_in_dim(doc_starts, core, 0, keepdims=False)
        block_rows, grad_rows, large, little = micro(
            plan,
            where,
            mp_rank,
            stream,
            lambda come: reordered(after(pick, come), folded, "order"),
            starts_row,
            weights,
        )

        def returned(x):
            mine, other = x[:own_rows], flip(x[own_rows:], 1)
            return jnp.where(core == 0, jnp.stack([mine, other]), jnp.stack([other, mine]))

        block_all, grad_all = returned(block_rows), returned(grad_rows)
    else:
        where = jnp.stack([0 * seq_rank, seq_rank]).astype(jnp.int32)
        found = [
            micro(plan, where, 0, high(tokens[m]), lambda come, m=m: cotangent[m], doc_starts[m], weights)
            for m in range(micros)
        ]
        block_all = jnp.stack([f[0] for f in found])
        grad_all = jnp.stack([f[1] for f in found])
        large, little = jax.tree.map(lambda *x: sum(x), *[f[2:] for f in found])

    late, gate_up_grad, down_grad = large
    sum_gates, lines, gains = little
    return (
        block_all,
        grad_all,
        late[:channels].T,
        late[channels : 2 * channels].T,
        late[2 * channels :],
        gate_up_grad[:hidden].T,
        gate_up_grad[hidden:].T,
        down_grad,
        sum_gates[:, :, 0],
        sum_gates[:, :, 1],
        lines[:4],
        lines[4],
        lines[5],
        lines[6],
        gains[0],
        gains[1],
    )


def solution(mesh):
    return jax.shard_map(
        on_device,
        mesh=mesh,
        in_specs=(
            P(None, ("seq", "mp"), None),
            P(None, "seq", None),
            P("seq", "mp"),
            P("seq", "mp"),
            P("mp", "seq"),
            P("seq", "mp"),
            P("seq", "mp"),
            P("mp", "seq"),
            P("mp", "seq", None),
            P("mp", "seq", None),
            P(None, ("mp", "seq")),
            P(("mp", "seq")),
            P(("mp", "seq")),
            P(("mp", "seq")),
            P("seq"),
            P("seq"),
            P(),
        ),
        out_specs=(
            P(None, ("seq", "mp"), None),
            P(None, ("seq", "mp"), None),
            P("seq", "mp"),
            P("seq", "mp"),
            P("mp", "seq"),
            P("seq", "mp"),
            P("seq", "mp"),
            P("mp", "seq"),
            P("mp", "seq", None),
            P("mp", "seq", None),
            P(None, ("mp", "seq")),
            P(("mp", "seq")),
            P(("mp", "seq")),
            P(("mp", "seq")),
            P("seq"),
            P("seq"),
        ),
        check_vma=False,
    )
```
